32 devices in a mesh: col: 4 (over z), dp: 8 (over y, x, core).
Axes of the slice: x: 2, y: 2, z: 4, core: 2. Of those that a mesh axis runs over, the one named last changes fastest.
Arguments:
- tokens: bfloat16 [512, 8192], P('col', 'dp'), may hold values from -6 to 6
- cotangent: bfloat16 [512, 8192], P('col', 'dp'), may hold values from -0.1796875 to 0.1796875
- gate_weight: bfloat16 [8192, 14336], P('dp', 'col'), may hold values from -0.09375 to 0.09375
- up_weight: bfloat16 [8192, 14336], P('dp', 'col'), may hold values from -0.09375 to 0.09375
- down_weight: bfloat16 [14336, 8192], P('col', 'dp'), may hold values from -0.0625 to 0.0625
- gate_mask: int32 [64, 112], P('dp', 'col'), may hold values 0 or 1
- up_mask: int32 [64, 112], P('dp', 'col'), may hold values 0 or 1
- down_mask: int32 [112, 64], P('col', 'dp'), may hold values 0 or 1
- counts: int32 [4], P('col'), may hold values from 1 to 128, 384 in all
Outputs:
- output: bfloat16 [512, 8192], P('col', 'dp')
- gate_grad: float32 [8192, 14336], P('dp', 'col')
- up_grad: float32 [8192, 14336], P('dp', 'col')
- down_grad: float32 [14336, 8192], P('col', 'dp')
The draws below stay inside these ranges and needn't reach their ends.
Inputs may be any that keep to these rules, and one draw needn't show every extreme that they name: `counts`: the largest count equals 128.
All inputs are finite; a program needn't handle non-finite values. No bound on the sum of `gate_mask` or of `up_mask` or of `down_mask` or of `counts` on one device may be relied on, other than what follows from the above.
Results may differ from the reference program's by a relative error of at most 0.039.
Values may be sent and summed in bfloat16 or wider, within the bound.
A program may use at most 192 MiB of HBM per device.

```python
import math
import jax
import jax.numpy as jnp
import numpy as np
from jax import lax

D = 8192
FF = 14336
BLOCK = 128
TOK_DEV = 128
TOKENS = 512
N_COL = 4
N_DP = 8


def with_ends(values, own_key, least, high):
    dims = values.shape
    spot = [jax.random.randint(jax.random.fold_in(own_key, axis), (), 0, dims[axis]) for axis in range(len(dims))]
    values = values.at[tuple(spot)].set(least)
    longest = dims.index(max(dims))
    spot[longest] = (spot[longest] + 1) % dims[longest]
    return values.at[tuple(spot)].set(high)


def steps_of(rng, dims, pieces, smallest, high):
    def one(axis_at, shards_of):
        steps = jax.random.uniform(jax.random.fold_in(jax.random.fold_in(rng, 6), axis_at), (shards_of,), jnp.float32, smallest / len(pieces), high / len(pieces))
        return jnp.repeat(jnp.exp(steps), dims[axis_at] // shards_of).reshape((-1,) + (1,) * (len(dims) - axis_at - 1))

    gain = one(*pieces[0])
    for cut in pieces[1:]:
        gain = gain * one(*cut)
    return gain


def profile(count, total, most, slope):
    weights = [(1 << 20) // math.isqrt(grade ** slope) + 1 for grade in range(2, count + 1)]
    rest, holding = total - most - (count - 1), [1] * (count - 1)
    while rest > 0:
        movable = [i for i in range(count - 1) if holding[i] < most]
        pool, budget = sum([weights[i] for i in movable]), rest
        for i in movable:
            more = min(most - holding[i], max(1, budget * weights[i] // pool), rest)
            holding[i] = holding[i] + more
            rest = rest - more
    return np.array([most] + holding)


def uneven(stream_key, number_of, total, reach, slope):
    if number_of == 2:
        one = jax.random.randint(stream_key, (), max(1, total - reach), min(reach, total - 1) + 1)
        return jnp.stack([one, total - one])
    tallies = jnp.asarray(profile(number_of, total, reach, slope), jnp.int32)
    couples = (number_of - 1) // 2
    giver, receiver = tallies[1:1 + 2 * couples:2], tallies[2:2 + 2 * couples:2]
    margin = jnp.minimum(giver - 1, reach - receiver)
    passed = jax.random.randint(jax.random.fold_in(stream_key, 1), (couples,), 0, 1 << 20) % (margin + 1)
    tallies = tallies.at[1:1 + 2 * couples:2].set(giver - passed).at[2:2 + 2 * couples:2].set(receiver + passed)
    return tallies[jax.random.permutation(jax.random.fold_in(stream_key, 2), number_of)]


def normal_values(rng, shape, deviation, reach, cuts=(), kind=jnp.bfloat16):
    drawn = jax.random.normal(rng, shape, jnp.float32) * deviation
    if len(cuts) > 0:
        drawn = steps_of(rng, shape, cuts, -0.22, 0.18) * drawn
    return jnp.clip(drawn, min=-reach, max=reach).astype(kind)


def setup_inputs(seed: int = 0) -> dict:
    keys = jax.random.split(jax.random.key(seed), 10)
    return {
        "tokens": normal_values(keys[0], (TOKENS, D), 1.0, 6.0, ((0, 4), (1, 8))),
        "cotangent": normal_values(keys[1], (TOKENS, D), 0.03, 0.1796875, ((0, 4), (1, 8))),
        "gate_weight": normal_values(keys[2], (D, FF), (D // 2) ** -0.5, 0.09375, ((0, 8), (1, 4))),
        "up_weight": normal_values(keys[3], (D, FF), (D // 2) ** -0.5, 0.09375, ((0, 8), (1, 4))),
        "down_weight": normal_values(keys[4], (FF, D), (FF // 2) ** -0.5, 0.0625, ((0, 4), (1, 8))),
        "gate_mask": with_ends((jax.random.randint(keys[5], (D // BLOCK, FF // BLOCK), 0, 2) < 1).astype(jnp.int32), jax.random.fold_in(keys[5], 1), 0, 1),
        "up_mask": with_ends((jax.random.randint(keys[6], (D // BLOCK, FF // BLOCK), 0, 2) < 1).astype(jnp.int32), jax.random.fold_in(keys[6], 1), 0, 1),
        "down_mask": with_ends((jax.random.randint(keys[7], (FF // BLOCK, D // BLOCK), 0, 2) < 1).astype(jnp.int32), jax.random.fold_in(keys[7], 1), 0, 1),
        "counts": uneven(keys[8], N_COL, TOK_DEV * N_COL * 3 // 4, TOK_DEV, 2).astype(jnp.int32),
    }


def expand(mask):
    wide = jnp.repeat(jnp.repeat(mask, BLOCK, axis=0), BLOCK, axis=1)
    return wide


def grouped(left, right, groups):
    width = left.shape[1] // groups
    total = jnp.zeros((left.shape[0], right.shape[1]), jnp.float32)
    for index in range(groups):
        piece = jnp.dot(left[:, index * width:(index + 1) * width], right[index * width:(index + 1) * width], preferred_element_type=jnp.float32)
        rounded = lax.optimization_barrier(piece.astype(jnp.bfloat16))
        total = total + rounded.astype(jnp.float32)
    return total


def reference(tokens, cotangent, gate_weight, up_weight, down_weight, gate_mask, up_mask, down_mask, counts):
    slots = jnp.arange(TOKENS, dtype=jnp.int32)
    live = ((slots % TOK_DEV) < jnp.repeat(counts, TOK_DEV))[:, None]
    keep_gate = expand(gate_mask)
    keep_up = expand(up_mask)
    keep_down = expand(down_mask)
    w_gate = jnp.where(keep_gate > 0, gate_weight, jnp.zeros_like(gate_weight))
    w_up = jnp.where(keep_up > 0, up_weight, jnp.zeros_like(up_weight))
    w_down = jnp.where(keep_down > 0, down_weight, jnp.zeros_like(down_weight))
    g_live = jnp.where(live, cotangent, jnp.zeros_like(cotangent))
    gate = grouped(tokens, w_gate, N_DP)
    upward = grouped(tokens, w_up, N_DP)
    sigma = jax.nn.sigmoid(gate)
    active = gate * sigma
    hidden = (active * upward).astype(jnp.bfloat16)
    mixed = grouped(hidden, w_down, N_COL)
    output = jnp.where(live, mixed, jnp.zeros_like(mixed)).astype(jnp.bfloat16)
    back = grouped(g_live, w_down.T, N_DP)
    d_gate = (back * upward * sigma * (1.0 + gate * (1.0 - sigma))).astype(jnp.bfloat16)
    d_up = (back * active).astype(jnp.bfloat16)
    gate_grad = jnp.dot(tokens.T, d_gate, preferred_element_type=jnp.float32)
    up_grad = jnp.dot(tokens.T, d_up, preferred_element_type=jnp.float32)
    down_grad = jnp.dot(hidden.T, g_live, preferred_element_type=jnp.float32)
    gate_grad = jnp.where(keep_gate > 0, gate_grad, jnp.zeros_like(gate_grad))
    up_grad = jnp.where(keep_up > 0, up_grad, jnp.zeros_like(up_grad))
    down_grad = jnp.where(keep_down > 0, down_grad, jnp.zeros_like(down_grad))
    return (output, gate_grad, up_grad, down_grad)
```

```python
import functools

import jax
import jax.numpy as jnp
from jax import lax
from jax.experimental import pallas as pl
from jax.experimental.pallas import tpu as pltpu
from jax.sharding import PartitionSpec as P

MESH = pl.DeviceIdType.MESH
BLOCK = 128
F32 = jnp.float32
BF16 = jnp.bfloat16


class Plan:
    def __init__(self, n_col, n_dp, tok_dev, feats, units):
        self.n_col, self.n_dp, self.tok_dev, self.feats, self.units = n_col, n_dp, tok_dev, feats, units
        self.levels = n_dp.bit_length() - 1
        self.rows = n_col * tok_dev * 3 // 4
        self.piece = self.rows // n_dp
        half = units // 2
        self.wide = 256 if half % 256 == 0 else BLOCK
        self.per_path = half // self.wide
        self.chunks = 2 * self.per_path
        k = self.levels
        self.bits = [list(range(k)), [0] + list(range(k - 1, 0, -1))]
        self.orders = []
        for bits in self.bits:
            order = []
            for place in range(n_dp):
                owner = 0
                for level, bit in enumerate(bits):
                    if place >> (k - 1 - level) & 1:
                        owner |= 1 << bit
                order.append(owner)
            self.orders.append(order)


def bit_of(index, bit):
    return (index // (1 << bit)) % 2


def partner_of(index, bit):
    return index + (1 - 2 * bit_of(index, bit)) * (1 << bit)


def exchange_kernel(
    plan,
    cnt_ref, tok_ref, cot_ref, gate_mask, up_mask, down_mask, wg_hbm, wu_hbm, wd_hbm,
    out_ref, tokc, gc, hid_out, d_out,
    cnt_all, tok_all, cot_all, place, wg, wu, wd, w_sem,
    keep, s0, r0, s1, r1, bkeep, bs0, br0, bs1, br1,
    hid, dd, acc, zs, zr,
    ring_sem, gu_sem, bk_sem, hid_sem, d_sem, z_sem, out_sem,
):
    n_col, k, td, wide = plan.n_col, plan.levels, plan.tok_dev, plan.wide
    rows, piece, per, chunks = plan.rows, plan.piece, plan.per_path, plan.chunks
    col, dp = lax.axis_index("col"), lax.axis_index("dp")

    def remote(src, dst, sems, at, **to):
        return pltpu.make_async_remote_copy(
            src_ref=src,
            dst_ref=dst,
            send_sem=sems.at[(0, *at)],
            recv_sem=sems.at[(1, *at)],
            device_id=(to.get("col", col), to.get("dp", dp)),
            device_id_type=MESH,
        )

    def weight_copies(u):
        cols = pl.ds(pl.multiple_of(u * wide, wide), wide)
        return (
            pltpu.make_async_copy(wg_hbm.at[:, cols], wg.at[u], w_sem.at[0, u]),
            pltpu.make_async_copy(wu_hbm.at[:, cols], wu.at[u], w_sem.at[1, u]),
            pltpu.make_async_copy(wd_hbm.at[cols, :], wd.at[u], w_sem.at[2, u]),
        )

    @pl.loop(0, chunks)
    def _(u):
        for copy in weight_copies(u):
            copy.start()

    barrier = pltpu.get_barrier_semaphore()
    for bit in range(k):
        pl.semaphore_signal(
            barrier, inc=1, device_id=(col, partner_of(dp, bit)), device_id_type=MESH
        )
    for step in range(1, n_col):
        pl.semaphore_signal(
            barrier, inc=1, device_id=((col + step) % n_col, dp), device_id_type=MESH
        )
    pl.semaphore_wait(barrier, k + n_col - 1)

    cnt_all[col] = cnt_ref[...]
    tok_all[col] = tok_ref[...]
    live = lax.broadcasted_iota(jnp.int32, (td, plan.feats), 0) < cnt_ref[0:1, 0:1]
    cot_all[col] = jnp.where(live, cot_ref[...].astype(F32), 0.0).astype(BF16)

    def hop(bufs, way, step, name):
        first, last = bufs
        block = col - step if way == 0 else col + step
        to = col + 1 if way == 0 else col - 1
        return [
            remote(buf.at[block], buf.at[block], ring_sem, (first + i, way, step), col=to)
            for i, buf in enumerate(last)
        ]

    def sends(way, step):
        return (
            (col - step >= 0) & (col + 1 < n_col) if way == 0 else (col + step < n_col) & (col >= 1)
        )

    def receives(way, step):
        return col - 1 - step >= 0 if way == 0 else col + 1 + step < n_col

    def hop_start(bufs, step):
        for way in range(2):

            @pl.when(sends(way, step))
            def _():
                for copy in hop(bufs, way, step, "s"):
                    copy.start()

    def hop_wait_recv(bufs, step):
        for way in range(2):

            @pl.when(receives(way, step))
            def _():
                first, last = bufs
                block = col - 1 - step if way == 0 else col + 1 + step
                for i, buf in enumerate(last):
                    remote(
                        buf.at[block], buf.at[block], ring_sem, (first + i, way, step), col=block
                    ).wait_recv()

    def hop_wait_send(bufs, step):
        for way in range(2):

            @pl.when(sends(way, step))
            def _():
                for copy in hop(bufs, way, step, "w"):
                    copy.wait_send()

    tok_bufs = (0, [tok_all, cnt_all])
    cot_bufs = (2, [cot_all])
    hop_start(tok_bufs, 0)

    side, parts = plan.feats // BLOCK, wide // BLOCK

    @pl.loop(0, chunks)
    def _(u):
        for copy in weight_copies(u):
            copy.wait()
        for r in range(side):
            for c in range(parts):
                at = (u, pl.ds(r * BLOCK, BLOCK), pl.ds(c * BLOCK, BLOCK))
                turned = (u, pl.ds(c * BLOCK, BLOCK), pl.ds(r * BLOCK, BLOCK))
                wg[at] = wg[at] * (gate_mask[r, u * parts + c] > 0).astype(F32).astype(BF16)
                wu[at] = wu[at] * (up_mask[r, u * parts + c] > 0).astype(F32).astype(BF16)
                wd[turned] = wd[turned] * (down_mask[u * parts + c, r] > 0).astype(F32).astype(BF16)

    for step in range(1, n_col - 1):
        hop_wait_recv(tok_bufs, step - 1)
        hop_start(tok_bufs, step)
    hop_wait_recv(tok_bufs, n_col - 2)
    hop_start(cot_bufs, 0)

    lane = lax.broadcasted_iota(jnp.int32, (piece, td), 1)
    row = lax.broadcasted_iota(jnp.int32, (piece, td), 0)
    before = jnp.zeros((1, td), jnp.int32)
    for shard in range(n_col):
        count = cnt_all[shard][0:1, :]
        for path in range(2):
            for i, owner in enumerate(plan.orders[path]):
                target = 0
                for bit in range(k):
                    mine = bit_of(dp, bit)
                    target = target + (1 - mine if owner >> bit & 1 else mine) * (1 << bit)
                hit = (row + target * piece - before == lane) & (lane < count)
                place[path, i * piece : (i + 1) * piece, shard * td : (shard + 1) * td] = jnp.where(
                    hit, 1.0, 0.0
                ).astype(BF16)
        before = before + count

    def compact(buf, to):
        for path in range(2):
            total = None
            for shard in range(n_col):
                part = jnp.dot(
                    place[path, :, shard * td : (shard + 1) * td],
                    buf[shard],
                    preferred_element_type=F32,
                )
                total = part if total is None else total + part
            to[path] = total.astype(BF16)

    compact(tok_all, tokc)

    class Scatter:
        def __init__(self, keep, s0, r0, s1, r1, sem):
            self.keep, self.bufs, self.sem = keep, ((s0, r0), (s1, r1)), sem

        def copy(self, path, level, u):
            size = rows >> (level + 1)
            src, dst = self.bufs[min(level, 1)]
            start = 0 if level == 0 else (rows >> 1) - (rows >> level)
            at = (u, pl.ds(start, size))
            return remote(
                src.at[at], dst.at[at], self.sem, (level, u),
                dp=partner_of(dp, plan.bits[path][level]),
            )

        def put(self, path, u, value):
            half = rows >> 1
            src, _ = self.bufs[0]
            src[u] = value[half:].astype(BF16)
            self.keep[u] = value[:half]
            self.copy(path, 0, u).start()

        def got(self, path, level, u):
            copy = self.copy(path, level, u)
            copy.wait_recv()
            size = rows >> (level + 1)
            _, dst = self.bufs[min(level, 1)]
            start = 0 if level == 0 else (rows >> 1) - (rows >> level)
            return self.keep[u, 0:size] + dst[u, pl.ds(start, size)].astype(F32)

        def step(self, path, level, u):
            value = self.got(path, level - 1, u)
            size = rows >> (level + 1)
            start = (rows >> 1) - (rows >> level)
            src, _ = self.bufs[1]
            src[u, pl.ds(start, size)] = value[size:].astype(BF16)
            self.keep[u, 0:size] = value[:size]
            self.copy(path, level, u).start()

    gu = Scatter(keep, s0, r0, s1, r1, gu_sem)
    bk = Scatter(bkeep, bs0, br0, bs1, br1, bk_sem)

    def gather_copy(buf, sem, path, level, u):
        size = rows >> (level + 1)
        return remote(
            buf.at[u, pl.ds(0, size)], buf.at[u, pl.ds(size, size)], sem, (level, u),
            dp=partner_of(dp, plan.bits[path][level]),
        )

    def both(body):
        for path in range(2):
            body(path)

    @pl.loop(0, per)
    def _(j):
        for path in range(2):
            u = path * per + j
            left = tokc[path]
            value = jnp.concatenate(
                [
                    jnp.dot(left, wg[u], preferred_element_type=F32),
                    jnp.dot(left, wu[u], preferred_element_type=F32),
                ],
                axis=1,
            )
            gu.put(path, u, value)

        @pl.when(j >= 1)
        def _():
            for path in range(2):
                gu.step(path, 1, path * per + j - 1)

    for path in range(2):
        gu.step(path, 1, path * per + per - 1)

    for step in range(1, n_col - 1):
        hop_wait_recv(cot_bufs, step - 1)
        hop_start(cot_bufs, step)
    if k > 2:

        @pl.loop(0, per)
        def _(j):
            for path in range(2):
                gu.step(path, 2, path * per + j)

    hop_wait_recv(cot_bufs, n_col - 2)
    compact(cot_all, gc)

    @pl.loop(0, per)
    def _(j):
        for path in range(2):
            u = path * per + j
            value = lax.dot_general(
                gc[path], wd[u], (((1,), (1,)), ((), ())), preferred_element_type=F32
            )
            bk.put(path, u, value)

        @pl.when(j >= 1)
        def _():
            for path in range(2):
                bk.step(path, 1, path * per + j - 1)

    for path in range(2):
        bk.step(path, 1, path * per + per - 1)

    for level in range(3, k):

        @pl.loop(0, per)
        def _(j):
            for path in range(2):
                gu.step(path, level, path * per + j)

    @pl.loop(0, per)
    def _(j):
        for path in range(2):
            u = path * per + j
            value = gu.got(path, k - 1, u)
            keep[u, 0:piece] = value
            gate, upward = value[:, :wide], value[:, wide:]
            sigma = 1.0 / (1.0 + jnp.exp(-gate))
            hid[u, 0:piece] = (gate * sigma * upward).astype(BF16)
            gather_copy(hid, hid_sem, path, k - 1, u).start()

    for level in range(2, k):

        @pl.loop(0, per)
        def _(j):
            for path in range(2):
                bk.step(path, level, path * per + j)

    def gather_step(buf, sem, level):
        @pl.loop(0, per)
        def _(j):
            for path in range(2):
                u = path * per + j
                gather_copy(buf, sem, path, level + 1, u).wait_recv()
                gather_copy(buf, sem, path, level, u).start()

    gather_step(hid, hid_sem, k - 2)

    @pl.loop(0, per)
    def _(j):
        for path in range(2):
            u = path * per + j
            back = bk.got(path, k - 1, u)
            gate, upward = keep[u, 0:piece, 0:wide], keep[u, 0:piece, wide : 2 * wide]
            sigma = 1.0 / (1.0 + jnp.exp(-gate))
            dd[u, 0:piece, 0:wide] = (
                back * upward * sigma * (1.0 + gate * (1.0 - sigma))
            ).astype(BF16)
            dd[u, 0:piece, wide : 2 * wide] = (back * (gate * sigma)).astype(BF16)
            gather_copy(dd, d_sem, path, k - 1, u).start()

    for level in range(k - 3, -1, -1):
        gather_step(hid, hid_sem, level)
    gather_step(dd, d_sem, k - 2)

    acc[...] = jnp.zeros_like(acc)

    @pl.loop(0, per)
    def _(j):
        for path in range(2):
            u = path * per + j
            gather_copy(hid, hid_sem, path, 0, u).wait_recv()
            pltpu.make_async_copy(hid.at[u], hid_out.at[u], out_sem.at[0, u]).start()
            acc[path] += jnp.dot(hid[u], wd[u], preferred_element_type=F32)

    for i, owner in enumerate(plan.orders[0]):
        other = plan.orders[1].index(owner)
        at = pl.ds(i * piece, piece)
        acc[0, at] = acc[0, at] + acc[1, pl.ds(other * piece, piece)]
    mixed = acc[0].astype(BF16)
    for shard in range(n_col):
        zs[shard] = lax.dot_general(
            place[0, :, shard * td : (shard + 1) * td],
            mixed,
            (((0,), (0,)), ((), ())),
            preferred_element_type=F32,
        ).astype(BF16)

    def z_copy(step):
        to = (col + step) % n_col
        return remote(zs.at[to], zr.at[step - 1], z_sem, (step - 1,), col=to)

    for step in range(1, n_col):
        z_copy(step).start()

    for level in range(k - 3, -1, -1):
        gather_step(dd, d_sem, level)

    @pl.loop(0, per)
    def _(j):
        for path in range(2):
            u = path * per + j
            gather_copy(dd, d_sem, path, 0, u).wait_recv()
            pltpu.make_async_copy(dd.at[u], d_out.at[u], out_sem.at[1, u]).start()

    total = zs[col].astype(F32)
    for step in range(1, n_col):
        z_copy(step).wait_recv()
        total = total + zr[step - 1].astype(F32)
    out_ref[...] = total.astype(BF16)

    for step in range(1, n_col):
        z_copy(step).wait_send()
    for step in range(n_col - 1):
        hop_wait_send(tok_bufs, step)
        hop_wait_send(cot_bufs, step)

    @pl.loop(0, per)
    def _(j):
        for path in range(2):
            u = path * per + j
            for level in range(k):
                gu.copy(path, level, u).wait_send()
                bk.copy(path, level, u).wait_send()
                gather_copy(hid, hid_sem, path, level, u).wait_send()
                gather_copy(dd, d_sem, path, level, u).wait_send()
            pltpu.make_async_copy(hid.at[u], hid_out.at[u], out_sem.at[0, u]).wait()
            pltpu.make_async_copy(dd.at[u], d_out.at[u], out_sem.at[1, u]).wait()


def exchange(plan, cnt, tokens, cotangent, gate_mask, up_mask, down_mask, wg, wu, wd):
    n_col, k, td, wide = plan.n_col, plan.levels, plan.tok_dev, plan.wide
    rows, chunks, feats = plan.rows, plan.chunks, plan.feats
    vmem, smem = pl.BlockSpec(memory_space=pltpu.VMEM), pl.BlockSpec(memory_space=pltpu.SMEM)
    whole = pl.BlockSpec(memory_space=pl.ANY)
    half = rows // 2
    rest = half - (rows >> k)

    def scatter_bufs(width):
        return [
            pltpu.VMEM((chunks, half, width), F32),
            pltpu.VMEM((chunks, half, width), BF16),
            pltpu.VMEM((chunks, half, width), BF16),
            pltpu.VMEM((chunks, rest, width), BF16),
            pltpu.VMEM((chunks, rest, width), BF16),
        ]

    return pl.pallas_call(
        functools.partial(exchange_kernel, plan),
        out_shape=(
            jax.ShapeDtypeStruct((td, feats), BF16),
            jax.ShapeDtypeStruct((2, rows, feats), BF16),
            jax.ShapeDtypeStruct((2, rows, feats), BF16),
            jax.ShapeDtypeStruct((chunks, rows, wide), BF16),
            jax.ShapeDtypeStruct((chunks, rows, 2 * wide), BF16),
        ),
        in_specs=[vmem, vmem, vmem, smem, smem, smem, whole, whole, whole],
        out_specs=(vmem, vmem, vmem, whole, whole),
        scratch_shapes=[
            pltpu.VMEM((n_col, 8, 128), jnp.int32),
            pltpu.VMEM((n_col, td, feats), BF16),
            pltpu.VMEM((n_col, td, feats), BF16),
            pltpu.VMEM((2, rows, n_col * td), BF16),
            pltpu.VMEM((chunks, feats, wide), BF16),
            pltpu.VMEM((chunks, feats, wide), BF16),
            pltpu.VMEM((chunks, wide, feats), BF16),
            pltpu.SemaphoreType.DMA((3, chunks)),
            *scatter_bufs(2 * wide),
            *scatter_bufs(wide),
            pltpu.VMEM((chunks, rows, wide), BF16),
            pltpu.VMEM((chunks, rows, 2 * wide), BF16),
            pltpu.VMEM((2, rows, feats), F32),
            pltpu.VMEM((n_col, td, feats), BF16),
            pltpu.VMEM((n_col - 1, td, feats), BF16),
            pltpu.SemaphoreType.DMA((2, 3, 2, n_col - 1)),
            pltpu.SemaphoreType.DMA((2, k, chunks)),
            pltpu.SemaphoreType.DMA((2, k, chunks)),
            pltpu.SemaphoreType.DMA((2, k, chunks)),
            pltpu.SemaphoreType.DMA((2, k, chunks)),
            pltpu.SemaphoreType.DMA((2, n_col - 1)),
            pltpu.SemaphoreType.DMA((2, chunks)),
        ],
        compiler_params=pltpu.CompilerParams(
            collective_id=0, has_side_effects=True, vmem_limit_bytes=63 * 2**20
        ),
    )(cnt, tokens, cotangent, gate_mask, up_mask, down_mask, wg, wu, wd)


def grads_kernel(
    plan, gate_mask, up_mask, down_mask, tokc, gc, hid, dd, gate_grad, up_grad, down_grad, turned
):
    u = pl.program_id(0)
    wide = plan.wide
    side, parts = plan.feats // BLOCK, wide // BLOCK

    @pl.when((u == 0) | (u == plan.per_path))
    def _():
        turned[...] = tokc[0].T

    def keep(mask, value):
        return jnp.where(mask > 0, value, 0.0)

    for ref, mask, lo in ((gate_grad, gate_mask, 0), (up_grad, up_mask, wide)):
        value = jnp.dot(turned[...], dd[0, :, lo : lo + wide], preferred_element_type=F32)
        for r in range(side):
            for c in range(parts):
                rs, cs = slice(r * BLOCK, (r + 1) * BLOCK), slice(c * BLOCK, (c + 1) * BLOCK)
                ref[rs, cs] = keep(mask[r, u * parts + c], value[rs, cs])
    value = jnp.dot(hid[0].T, gc[0], preferred_element_type=F32)
    for r in range(side):
        for c in range(parts):
            rs, cs = slice(r * BLOCK, (r + 1) * BLOCK), slice(c * BLOCK, (c + 1) * BLOCK)
            down_grad[cs, rs] = keep(down_mask[u * parts + c, r], value[cs, rs])


def grads(plan, gate_mask, up_mask, down_mask, tokc, gc, hid, dd):
    rows, feats, wide, per = plan.rows, plan.feats, plan.wide, plan.per_path
    smem = pl.BlockSpec(memory_space=pltpu.SMEM)
    return pl.pallas_call(
        functools.partial(grads_kernel, plan),
        grid=(plan.chunks,),
        out_shape=(
            jax.ShapeDtypeStruct((feats, plan.units), F32),
            jax.ShapeDtypeStruct((feats, plan.units), F32),
            jax.ShapeDtypeStruct((plan.units, feats), F32),
        ),
        in_specs=[
            smem,
            smem,
            smem,
            pl.BlockSpec((1, rows, feats), lambda u: (u // per, 0, 0)),
            pl.BlockSpec((1, rows, feats), lambda u: (u // per, 0, 0)),
            pl.BlockSpec((1, rows, wide), lambda u: (u, 0, 0)),
            pl.BlockSpec((1, rows, 2 * wide), lambda u: (u, 0, 0)),
        ],
        out_specs=(
            pl.BlockSpec((feats, wide), lambda u: (0, u)),
            pl.BlockSpec((feats, wide), lambda u: (0, u)),
            pl.BlockSpec((wide, feats), lambda u: (u, 0)),
        ),
        scratch_shapes=[pltpu.VMEM((feats, rows), BF16)],
        compiler_params=pltpu.CompilerParams(vmem_limit_bytes=48 * 2**20),
    )(gate_mask, up_mask, down_mask, tokc, gc, hid, dd)


def on_device(
    n_col, n_dp,
    tokens, cotangent, gate_weight, up_weight, down_weight, gate_mask, up_mask, down_mask, counts
):
    plan = Plan(n_col, n_dp, tokens.shape[0], tokens.shape[1], gate_weight.shape[1])
    cnt = jnp.broadcast_to(counts.reshape(1, 1), (8, 128))
    output, tokc, gc, hid, dd = exchange(
        plan, cnt, tokens, cotangent, gate_mask, up_mask, down_mask,
        gate_weight, up_weight, down_weight,
    )
    gate_grad, up_grad, down_grad = grads(plan, gate_mask, up_mask, down_mask, tokc, gc, hid, dd)
    return (output, gate_grad, up_grad, down_grad)


def solution(mesh):
    in_specs = (
        P("col", "dp"),
        P("col", "dp"),
        P("dp", "col"),
        P("dp", "col"),
        P("col", "dp"),
        P("dp", "col"),
        P("dp", "col"),
        P("col", "dp"),
        P("col"),
    )
    out_specs = (P("col", "dp"), P("dp", "col"), P("dp", "col"), P("col", "dp"))
    return jax.shard_map(
        functools.partial(on_device, mesh.shape["col"], mesh.shape["dp"]),
        mesh=mesh,
        in_specs=in_specs,
        out_specs=out_specs,
        check_vma=False,
    )
```

```python
import functools

import jax
import jax.numpy as jnp
from jax import lax
from jax.experimental import pallas as pl
from jax.experimental.pallas import tpu as pltpu
from jax.sharding import PartitionSpec as P

MESH = pl.DeviceIdType.MESH
BLOCK = 128
F32 = jnp.float32
BF16 = jnp.bfloat16


class Plan:
    def __init__(self, n_col, n_dp, tok_dev, feats, units):
        self.n_col, self.n_dp, self.tok_dev, self.feats, self.units = n_col, n_dp, tok_dev, feats, units
        self.levels = n_dp.bit_length() - 1
        self.rows = n_col * tok_dev * 3 // 4
        self.piece = self.rows // n_dp
        half = units // 2
        self.wide = 256 if half % 256 == 0 else BLOCK
        self.per_path = half // self.wide
        self.chunks = 2 * self.per_path
        k = self.levels
        self.bits = [list(range(k)), [0] + list(range(k - 1, 0, -1))]
        self.orders = []
        for bits in self.bits:
            order = []
            for place in range(n_dp):
                owner = 0
                for level, bit in enumerate(bits):
                    if place >> (k - 1 - level) & 1:
                        owner |= 1 << bit
                order.append(owner)
            self.orders.append(order)


def bit_of(index, bit):
    return (index // (1 << bit)) % 2


def partner_of(index, bit):
    return index + (1 - 2 * bit_of(index, bit)) * (1 << bit)


def exchange_kernel(
    plan,
    cnt_ref, tok_ref, cot_ref, gate_mask, up_mask, down_mask, wg_hbm, wu_hbm, wd_hbm,
    out_ref, tokc, gc, hid_out, d_out,
    cnt_all, tok_all, cot_all, place, wg, wu, wd, w_sem,
    keep, s0, r0, s1, r1, bkeep, bs0, br0, bs1, br1,
    hid, dd, acc, zs, zr,
    ring_sem, gu_sem, bk_sem, hid_sem, d_sem, z_sem, out_sem,
):
    n_col, k, td, wide = plan.n_col, plan.levels, plan.tok_dev, plan.wide
    rows, piece, per, chunks = plan.rows, plan.piece, plan.per_path, plan.chunks
    col, dp = lax.axis_index("col"), lax.axis_index("dp")

    def remote(src, dst, sems, at, **to):
        return pltpu.make_async_remote_copy(
            src_ref=src,
            dst_ref=dst,
            send_sem=sems.at[(0, *at)],
            recv_sem=sems.at[(1, *at)],
            device_id=(to.get("col", col), to.get("dp", dp)),
            device_id_type=MESH,
        )

    def weight_copies(u):
        cols = pl.ds(pl.multiple_of(u * wide, wide), wide)
        return (
            pltpu.make_async_copy(wg_hbm.at[:, cols], wg.at[u], w_sem.at[0, u]),
            pltpu.make_async_copy(wu_hbm.at[:, cols], wu.at[u], w_sem.at[1, u]),
            pltpu.make_async_copy(wd_hbm.at[cols, :], wd.at[u], w_sem.at[2, u]),
        )

    @pl.loop(0, chunks)
    def _(u):
        for copy in weight_copies(u)[:2]:
            copy.start()

    @pl.loop(0, chunks)
    def _(u):
        weight_copies(u)[2].start()

    barrier = pltpu.get_barrier_semaphore()
    for bit in range(k):
        pl.semaphore_signal(
            barrier, inc=1, device_id=(col, partner_of(dp, bit)), device_id_type=MESH
        )
    for step in range(1, n_col):
        pl.semaphore_signal(
            barrier, inc=1, device_id=((col + step) % n_col, dp), device_id_type=MESH
        )
    pl.semaphore_wait(barrier, k + n_col - 1)

    cnt_all[col] = cnt_ref[...]
    tok_all[col] = tok_ref[...]
    live = lax.broadcasted_iota(jnp.int32, (td, plan.feats), 0) < cnt_ref[0:1, 0:1]
    cot_all[col] = jnp.where(live, cot_ref[...].astype(F32), 0.0).astype(BF16)

    def hop(bufs, way, step, name):
        first, last = bufs
        block = col - step if way == 0 else col + step
        to = col + 1 if way == 0 else col - 1
        return [
            remote(buf.at[block], buf.at[block], ring_sem, (first + i, way, step), col=to)
            for i, buf in enumerate(last)
        ]

    def sends(way, step):
        return (
            (col - step >= 0) & (col + 1 < n_col) if way == 0 else (col + step < n_col) & (col >= 1)
        )

    def receives(way, step):
        return col - 1 - step >= 0 if way == 0 else col + 1 + step < n_col

    def hop_start(bufs, step):
        for way in range(2):

            @pl.when(sends(way, step))
            def _():
                for copy in hop(bufs, way, step, "s"):
                    copy.start()

    def hop_wait_recv(bufs, step):
        for way in range(2):

            @pl.when(receives(way, step))
            def _():
                first, last = bufs
                block = col - 1 - step if way == 0 else col + 1 + step
                for i, buf in enumerate(last):
                    remote(
                        buf.at[block], buf.at[block], ring_sem, (first + i, way, step), col=block
                    ).wait_recv()

    def hop_wait_send(bufs, step):
        for way in range(2):

            @pl.when(sends(way, step))
            def _():
                for copy in hop(bufs, way, step, "w"):
                    copy.wait_send()

    tok_bufs = (0, [tok_all, cnt_all])
    cot_bufs = (2, [cot_all])
    hop_start(tok_bufs, 0)

    side, parts = plan.feats // BLOCK, wide // BLOCK

    def prune_in(lo, hi):
        @pl.loop(lo, hi)
        def _(u):
            for copy in weight_copies(u)[:2]:
                copy.wait()
            for r in range(side):
                for c in range(parts):
                    at = (u, pl.ds(r * BLOCK, BLOCK), pl.ds(c * BLOCK, BLOCK))
                    wg[at] = wg[at] * (gate_mask[r, u * parts + c] > 0).astype(F32).astype(BF16)
                    wu[at] = wu[at] * (up_mask[r, u * parts + c] > 0).astype(F32).astype(BF16)

    def prune_down():
        @pl.loop(0, chunks)
        def _(u):
            weight_copies(u)[2].wait()
            for r in range(side):
                for c in range(parts):
                    at = (u, pl.ds(c * BLOCK, BLOCK), pl.ds(r * BLOCK, BLOCK))
                    wd[at] = wd[at] * (down_mask[r, u * parts + c] > 0).astype(F32).astype(BF16)

    prune_in(0, per)
    for step in range(1, n_col - 1):
        hop_wait_recv(tok_bufs, step - 1)
        hop_start(tok_bufs, step)
        if step == 1:
            prune_in(per, chunks)
    hop_wait_recv(tok_bufs, n_col - 2)
    hop_start(cot_bufs, 0)

    lane = lax.broadcasted_iota(jnp.int32, (piece, td), 1)
    row = lax.broadcasted_iota(jnp.int32, (piece, td), 0)
    before = jnp.zeros((1, td), jnp.int32)
    for shard in range(n_col):
        count = cnt_all[shard][0:1, :]
        for path in range(2):
            for i, owner in enumerate(plan.orders[path]):
                target = 0
                for bit in range(k):
                    mine = bit_of(dp, bit)
                    target = target + (1 - mine if owner >> bit & 1 else mine) * (1 << bit)
                hit = (row + target * piece - before == lane) & (lane < count)
                place[path, i * piece : (i + 1) * piece, shard * td : (shard + 1) * td] = jnp.where(
                    hit, 1.0, 0.0
                ).astype(BF16)
        before = before + count

    def compact(buf, to):
        for path in range(2):
            total = None
            for shard in range(n_col):
                part = jnp.dot(
                    place[path, :, shard * td : (shard + 1) * td],
                    buf[shard],
                    preferred_element_type=F32,
                )
                total = part if total is None else total + part
            to[path] = total.astype(BF16)

    compact(tok_all, tokc)

    class Scatter:
        def __init__(self, keep, s0, r0, s1, r1, sem):
            self.keep, self.bufs, self.sem = keep, ((s0, r0), (s1, r1)), sem

        def copy(self, path, level, u):
            size = rows >> (level + 1)
            src, dst = self.bufs[min(level, 1)]
            start = 0 if level == 0 else (rows >> 1) - (rows >> level)
            at = (u, pl.ds(start, size))
            return remote(
                src.at[at], dst.at[at], self.sem, (level, u),
                dp=partner_of(dp, plan.bits[path][level]),
            )

        def put(self, path, u, value):
            half = rows >> 1
            src, _ = self.bufs[0]
            src[u] = value[half:].astype(BF16)
            self.keep[u] = value[:half]
            self.copy(path, 0, u).start()

        def got(self, path, level, u):
            copy = self.copy(path, level, u)
            copy.wait_recv()
            size = rows >> (level + 1)
            _, dst = self.bufs[min(level, 1)]
            start = 0 if level == 0 else (rows >> 1) - (rows >> level)
            return self.keep[u, 0:size] + dst[u, pl.ds(start, size)].astype(F32)

        def step(self, path, level, u):
            value = self.got(path, level - 1, u)
            size = rows >> (level + 1)
            start = (rows >> 1) - (rows >> level)
            src, _ = self.bufs[1]
            src[u, pl.ds(start, size)] = value[size:].astype(BF16)
            self.keep[u, 0:size] = value[:size]
            self.copy(path, level, u).start()

    gu = Scatter(keep, s0, r0, s1, r1, gu_sem)
    bk = Scatter(bkeep, bs0, br0, bs1, br1, bk_sem)

    def gather_copy(buf, sem, path, level, u):
        size = rows >> (level + 1)
        return remote(
            buf.at[u, pl.ds(0, size)], buf.at[u, pl.ds(size, size)], sem, (level, u),
            dp=partner_of(dp, plan.bits[path][level]),
        )

    def both(body):
        for path in range(2):
            body(path)

    @pl.loop(0, per)
    def _(j):
        for path in range(2):
            u = path * per + j
            left = tokc[path]
            value = jnp.concatenate(
                [
                    jnp.dot(left, wg[u], preferred_element_type=F32),
                    jnp.dot(left, wu[u], preferred_element_type=F32),
                ],
                axis=1,
            )
            gu.put(path, u, value)

        @pl.when(j >= 1)
        def _():
            for path in range(2):
                gu.step(path, 1, path * per + j - 1)

    for path in range(2):
        gu.step(path, 1, path * per + per - 1)

    prune_down()

    for step in range(1, n_col - 1):
        hop_wait_recv(cot_bufs, step - 1)
        hop_start(cot_bufs, step)
    if k > 2:

        @pl.loop(0, per)
        def _(j):
            for path in range(2):
                gu.step(path, 2, path * per + j)

    hop_wait_recv(cot_bufs, n_col - 2)
    compact(cot_all, gc)

    @pl.loop(0, per)
    def _(j):
        for path in range(2):
            u = path * per + j
            value = lax.dot_general(
                gc[path], wd[u], (((1,), (1,)), ((), ())), preferred_element_type=F32
            )
            bk.put(path, u, value)

        @pl.when(j >= 1)
        def _():
            for path in range(2):
                bk.step(path, 1, path * per + j - 1)

    for path in range(2):
        bk.step(path, 1, path * per + per - 1)

    for level in range(3, k):

        @pl.loop(0, per)
        def _(j):
            for path in range(2):
                gu.step(path, level, path * per + j)

    @pl.loop(0, per)
    def _(j):
        for path in range(2):
            u = path * per + j
            value = gu.got(path, k - 1, u)
            keep[u, 0:piece] = value
            gate, upward = value[:, :wide], value[:, wide:]
            sigma = 1.0 / (1.0 + jnp.exp(-gate))
            hid[u, 0:piece] = (gate * sigma * upward).astype(BF16)
            gather_copy(hid, hid_sem, path, k - 1, u).start()

    def gather_step(buf, sem, level):
        @pl.loop(0, per)
        def _(j):
            for path in range(2):
                u = path * per + j
                gather_copy(buf, sem, path, level + 1, u).wait_recv()
                gather_copy(buf, sem, path, level, u).start()

    gather_step(hid, hid_sem, k - 2)

    for level in range(2, k):

        @pl.loop(0, per)
        def _(j):
            for path in range(2):
                bk.step(path, level, path * per + j)

    for level in range(k - 3, -1, -1):
        gather_step(hid, hid_sem, level)

    @pl.loop(0, per)
    def _(j):
        for path in range(2):
            u = path * per + j
            back = bk.got(path, k - 1, u)
            gate, upward = keep[u, 0:piece, 0:wide], keep[u, 0:piece, wide : 2 * wide]
            sigma = 1.0 / (1.0 + jnp.exp(-gate))
            dd[u, 0:piece, 0:wide] = (
                back * upward * sigma * (1.0 + gate * (1.0 - sigma))
            ).astype(BF16)
            dd[u, 0:piece, wide : 2 * wide] = (back * (gate * sigma)).astype(BF16)
            gather_copy(dd, d_sem, path, k - 1, u).start()

    acc[...] = jnp.zeros_like(acc)

    @pl.loop(0, per)
    def _(j):
        for path in range(2):
            u = path * per + j
            gather_copy(hid, hid_sem, path, 0, u).wait_recv()
            pltpu.make_async_copy(hid.at[u], hid_out.at[u], out_sem.at[0, u]).start()
            acc[path] += jnp.dot(hid[u], wd[u], preferred_element_type=F32)

    for i, owner in enumerate(plan.orders[0]):
        other = plan.orders[1].index(owner)
        at = pl.ds(i * piece, piece)
        acc[0, at] = acc[0, at] + acc[1, pl.ds(other * piece, piece)]
    mixed = acc[0].astype(BF16)
    for shard in range(n_col):
        zs[shard] = lax.dot_general(
            place[0, :, shard * td : (shard + 1) * td],
            mixed,
            (((0,), (0,)), ((), ())),
            preferred_element_type=F32,
        ).astype(BF16)

    def z_copy(step):
        to = (col + step) % n_col
        return remote(zs.at[to], zr.at[step - 1], z_sem, (step - 1,), col=to)

    for step in range(1, n_col):
        z_copy(step).start()

    for level in range(k - 2, -1, -1):
        gather_step(dd, d_sem, level)

    @pl.loop(0, per)
    def _(j):
        for path in range(2):
            u = path * per + j
            gather_copy(dd, d_sem, path, 0, u).wait_recv()
            pltpu.make_async_copy(dd.at[u], d_out.at[u], out_sem.at[1, u]).start()

    total = zs[col].astype(F32)
    for step in range(1, n_col):
        z_copy(step).wait_recv()
        total = total + zr[step - 1].astype(F32)
    out_ref[...] = total.astype(BF16)

    for step in range(1, n_col):
        z_copy(step).wait_send()
    for step in range(n_col - 1):
        hop_wait_send(tok_bufs, step)
        hop_wait_send(cot_bufs, step)

    @pl.loop(0, per)
    def _(j):
        for path in range(2):
            u = path * per + j
            for level in range(k):
                gu.copy(path, level, u).wait_send()
                bk.copy(path, level, u).wait_send()
                gather_copy(hid, hid_sem, path, level, u).wait_send()
                gather_copy(dd, d_sem, path, level, u).wait_send()
            pltpu.make_async_copy(hid.at[u], hid_out.at[u], out_sem.at[0, u]).wait()
            pltpu.make_async_copy(dd.at[u], d_out.at[u], out_sem.at[1, u]).wait()


def exchange(plan, cnt, tokens, cotangent, gate_mask, up_mask, down_mask, wg, wu, wd):
    n_col, k, td, wide = plan.n_col, plan.levels, plan.tok_dev, plan.wide
    rows, chunks, feats = plan.rows, plan.chunks, plan.feats
    vmem, smem = pl.BlockSpec(memory_space=pltpu.VMEM), pl.BlockSpec(memory_space=pltpu.SMEM)
    whole = pl.BlockSpec(memory_space=pl.ANY)
    half = rows // 2
    rest = half - (rows >> k)

    def scatter_bufs(width):
        return [
            pltpu.VMEM((chunks, half, width), F32),
            pltpu.VMEM((chunks, half, width), BF16),
            pltpu.VMEM((chunks, half, width), BF16),
            pltpu.VMEM((chunks, rest, width), BF16),
            pltpu.VMEM((chunks, rest, width), BF16),
        ]

    return pl.pallas_call(
        functools.partial(exchange_kernel, plan),
        out_shape=(
            jax.ShapeDtypeStruct((td, feats), BF16),
            jax.ShapeDtypeStruct((2, rows, feats), BF16),
            jax.ShapeDtypeStruct((2, rows, feats), BF16),
            jax.ShapeDtypeStruct((chunks, rows, wide), BF16),
            jax.ShapeDtypeStruct((chunks, rows, 2 * wide), BF16),
        ),
        in_specs=[vmem, vmem, vmem, smem, smem, smem, whole, whole, whole],
        out_specs=(vmem, vmem, vmem, whole, whole),
        scratch_shapes=[
            pltpu.VMEM((n_col, 8, 128), jnp.int32),
            pltpu.VMEM((n_col, td, feats), BF16),
            pltpu.VMEM((n_col, td, feats), BF16),
            pltpu.VMEM((2, rows, n_col * td), BF16),
            pltpu.VMEM((chunks, feats, wide), BF16),
            pltpu.VMEM((chunks, feats, wide), BF16),
            pltpu.VMEM((chunks, wide, feats), BF16),
            pltpu.SemaphoreType.DMA((3, chunks)),
            *scatter_bufs(2 * wide),
            *scatter_bufs(wide),
            pltpu.VMEM((chunks, rows, wide), BF16),
            pltpu.VMEM((chunks, rows, 2 * wide), BF16),
            pltpu.VMEM((2, rows, feats), F32),
            pltpu.VMEM((n_col, td, feats), BF16),
            pltpu.VMEM((n_col - 1, td, feats), BF16),
            pltpu.SemaphoreType.DMA((2, 3, 2, n_col - 1)),
            pltpu.SemaphoreType.DMA((2, k, chunks)),
            pltpu.SemaphoreType.DMA((2, k, chunks)),
            pltpu.SemaphoreType.DMA((2, k, chunks)),
            pltpu.SemaphoreType.DMA((2, k, chunks)),
            pltpu.SemaphoreType.DMA((2, n_col - 1)),
            pltpu.SemaphoreType.DMA((2, chunks)),
        ],
        compiler_params=pltpu.CompilerParams(
            collective_id=0, has_side_effects=True, vmem_limit_bytes=63 * 2**20
        ),
    )(cnt, tokens, cotangent, gate_mask, up_mask, down_mask, wg, wu, wd)


def grads_kernel(
    plan, gate_mask, up_mask, down_mask, tokc, gc, hid, dd, gate_grad, up_grad, down_grad, turned
):
    u = pl.program_id(0)
    wide = plan.wide
    side, parts = plan.feats // BLOCK, wide // BLOCK

    @pl.when((u == 0) | (u == plan.per_path))
    def _():
        turned[...] = tokc[0].T

    def keep(mask, value):
        return jnp.where(mask > 0, value, 0.0)

    for ref, mask, lo in ((gate_grad, gate_mask, 0), (up_grad, up_mask, wide)):
        value = jnp.dot(turned[...], dd[0, :, lo : lo + wide], preferred_element_type=F32)
        for r in range(side):
            for c in range(parts):
                rs, cs = slice(r * BLOCK, (r + 1) * BLOCK), slice(c * BLOCK, (c + 1) * BLOCK)
                ref[rs, cs] = keep(mask[r, u * parts + c], value[rs, cs])
    value = jnp.dot(hid[0].T, gc[0], preferred_element_type=F32)
    for r in range(side):
        for c in range(parts):
            rs, cs = slice(r * BLOCK, (r + 1) * BLOCK), slice(c * BLOCK, (c + 1) * BLOCK)
            down_grad[cs, rs] = keep(down_mask[r, u * parts + c], value[cs, rs])


def grads(plan, gate_mask, up_mask, down_mask, tokc, gc, hid, dd):
    rows, feats, wide, per = plan.rows, plan.feats, plan.wide, plan.per_path
    smem = pl.BlockSpec(memory_space=pltpu.SMEM)
    return pl.pallas_call(
        functools.partial(grads_kernel, plan),
        grid=(plan.chunks,),
        out_shape=(
            jax.ShapeDtypeStruct((feats, plan.units), F32),
            jax.ShapeDtypeStruct((feats, plan.units), F32),
            jax.ShapeDtypeStruct((plan.units, feats), F32),
        ),
        in_specs=[
            smem,
            smem,
            smem,
            pl.BlockSpec((1, rows, feats), lambda u: (u // per, 0, 0)),
            pl.BlockSpec((1, rows, feats), lambda u: (u // per, 0, 0)),
            pl.BlockSpec((1, rows, wide), lambda u: (u, 0, 0)),
            pl.BlockSpec((1, rows, 2 * wide), lambda u: (u, 0, 0)),
        ],
        out_specs=(
            pl.BlockSpec((feats, wide), lambda u: (0, u)),
            pl.BlockSpec((feats, wide), lambda u: (0, u)),
            pl.BlockSpec((wide, feats), lambda u: (u, 0)),
        ),
        scratch_shapes=[pltpu.VMEM((feats, rows), BF16)],
        compiler_params=pltpu.CompilerParams(vmem_limit_bytes=63 * 2**20),
    )(gate_mask, up_mask, down_mask, tokc, gc, hid, dd)


def on_device(
    n_col, n_dp,
    tokens, cotangent, gate_weight, up_weight, down_weight, gate_mask, up_mask, down_mask, counts
):
    plan = Plan(n_col, n_dp, tokens.shape[0], tokens.shape[1], gate_weight.shape[1])
    cnt = jnp.broadcast_to(counts.reshape(1, 1), (8, 128))
    down_mask = down_mask.T
    output, tokc, gc, hid, dd = exchange(
        plan, cnt, tokens, cotangent, gate_mask, up_mask, down_mask,
        gate_weight, up_weight, down_weight,
    )
    gate_grad, up_grad, down_grad = grads(plan, gate_mask, up_mask, down_mask, tokc, gc, hid, dd)
    return (output, gate_grad, up_grad, down_grad)


def solution(mesh):
    in_specs = (
        P("col", "dp"),
        P("col", "dp"),
        P("dp", "col"),
        P("dp", "col"),
        P("col", "dp"),
        P("dp", "col"),
        P("dp", "col"),
        P("col", "dp"),
        P("col"),
    )
    out_specs = (P("col", "dp"), P("dp", "col"), P("dp", "col"), P("col", "dp"))
    return jax.shard_map(
        functools.partial(on_device, mesh.shape["col"], mesh.shape["dp"]),
        mesh=mesh,
        in_specs=in_specs,
        out_specs=out_specs,
        check_vma=False,
    )
```

```python
import functools

import jax
import jax.numpy as jnp
from jax import lax
from jax.experimental import pallas as pl
from jax.experimental.pallas import tpu as pltpu
from jax.sharding import PartitionSpec as P

MESH = pl.DeviceIdType.MESH
BLOCK = 128
F32 = jnp.float32
BF16 = jnp.bfloat16


class Plan:
    def __init__(self, n_col, n_dp, tok_dev, feats, units):
        self.n_col, self.n_dp, self.tok_dev, self.feats, self.units = n_col, n_dp, tok_dev, feats, units
        self.levels = n_dp.bit_length() - 1
        self.rows = n_col * tok_dev * 3 // 4
        self.piece = self.rows // n_dp
        half = units // 2
        self.wide = 256 if half % 256 == 0 else BLOCK
        self.per_path = half // self.wide
        self.chunks = 2 * self.per_path
        k = self.levels
        self.bits = [list(range(k)), [0] + list(range(k - 1, 0, -1))]
        first, dead = 16 * n_dp, n_col * tok_dev - self.rows
        self.early = -(-(first + dead) // tok_dev) - 1
        self.sections = [first, self.rows - first]
        self.orders = []
        for bits in self.bits:
            order = []
            for place in range(n_dp):
                owner = 0
                for level, bit in enumerate(bits):
                    if place >> (k - 1 - level) & 1:
                        owner |= 1 << bit
                order.append(owner)
            self.orders.append(order)


def bit_of(index, bit):
    return (index // (1 << bit)) % 2


def partner_of(index, bit):
    return index + (1 - 2 * bit_of(index, bit)) * (1 << bit)


def exchange_kernel(
    plan,
    cnt_ref, tok_ref, cot_ref, gate_mask, up_mask, down_mask, wg_hbm, wu_hbm, wd_hbm,
    out_ref, tokc, d_out, down_out,
    cnt_all, tok_all, cot_all, gc, place0, place1, tok0, tok1, wg, wu, wd, w_sem,
    keep0, s00, r00, s10, r10, keep1, s01, r01, s11, r11, bkeep, bs0, br0, bs1, br1,
    hid, dd, acc, zs, zr, down,
    cnt_sem, ring_sem, gu0_sem, gu1_sem, bk_sem, hid_sem, d_sem, z_sem, out_sem, tok_sem,
):
    n_col, k, td, wide = plan.n_col, plan.levels, plan.tok_dev, plan.wide
    rows, piece, per, chunks = plan.rows, plan.piece, plan.per_path, plan.chunks
    col, dp = lax.axis_index("col"), lax.axis_index("dp")

    def remote(src, dst, sems, at, **to):
        return pltpu.make_async_remote_copy(
            src_ref=src,
            dst_ref=dst,
            send_sem=sems.at[(0, *at)],
            recv_sem=sems.at[(1, *at)],
            device_id=(to.get("col", col), to.get("dp", dp)),
            device_id_type=MESH,
        )

    def weight_copies(u):
        cols = pl.ds(pl.multiple_of(u * wide, wide), wide)
        return (
            pltpu.make_async_copy(wg_hbm.at[:, cols], wg.at[u], w_sem.at[0, u]),
            pltpu.make_async_copy(wu_hbm.at[:, cols], wu.at[u], w_sem.at[1, u]),
            pltpu.make_async_copy(wd_hbm.at[cols, :], wd.at[u], w_sem.at[2, u]),
        )

    @pl.loop(0, chunks)
    def _(u):
        for copy in weight_copies(u)[:2]:
            copy.start()

    @pl.loop(0, chunks)
    def _(u):
        weight_copies(u)[2].start()

    barrier = pltpu.get_barrier_semaphore()
    for bit in range(k):
        pl.semaphore_signal(
            barrier, inc=1, device_id=(col, partner_of(dp, bit)), device_id_type=MESH
        )
    for step in range(1, n_col):
        pl.semaphore_signal(
            barrier, inc=1, device_id=((col + step) % n_col, dp), device_id_type=MESH
        )
    pl.semaphore_wait(barrier, k + n_col - 1)

    cnt_all[col] = cnt_ref[...]
    tok_all[col] = tok_ref[...]
    live = lax.broadcasted_iota(jnp.int32, (td, plan.feats), 0) < cnt_ref[0:1, 0:1]
    cot_all[col] = jnp.where(live, cot_ref[...].astype(F32), 0.0).astype(BF16)

    def hop(bufs, way, step, name):
        first, last = bufs
        block = col - step if way == 0 else col + step
        to = col + 1 if way == 0 else col - 1
        return [
            remote(buf.at[block], buf.at[block], ring_sem, (first + i, way, step), col=to)
            for i, buf in enumerate(last)
        ]

    def sends(way, step):
        return (
            (col - step >= 0) & (col + 1 < n_col) if way == 0 else (col + step < n_col) & (col >= 1)
        )

    def receives(way, step):
        return col - 1 - step >= 0 if way == 0 else col + 1 + step < n_col

    def hop_start(bufs, step):
        for way in range(2):

            @pl.when(sends(way, step))
            def _():
                for copy in hop(bufs, way, step, "s"):
                    copy.start()

    def hop_wait_recv(bufs, step):
        for way in range(2):

            @pl.when(receives(way, step))
            def _():
                first, last = bufs
                block = col - 1 - step if way == 0 else col + 1 + step
                for i, buf in enumerate(last):
                    remote(
                        buf.at[block], buf.at[block], ring_sem, (first + i, way, step), col=block
                    ).wait_recv()

    def hop_wait_send(bufs, step):
        for way in range(2):

            @pl.when(sends(way, step))
            def _():
                for copy in hop(bufs, way, step, "w"):
                    copy.wait_send()

    def cnt_copy(step):
        to = (col + step) % n_col
        return remote(cnt_all.at[col], cnt_all.at[col], cnt_sem, (step - 1,), col=to)

    for step in range(1, n_col):
        cnt_copy(step).start()
    tok_bufs = (0, [tok_all])
    cot_bufs = (1, [cot_all])
    hop_start(tok_bufs, 0)

    side, parts = plan.feats // BLOCK, wide // BLOCK

    def prune_in(u):
        for copy in weight_copies(u)[:2]:
            copy.wait()
        for r in range(side):
            for c in range(parts):
                at = (u, pl.ds(r * BLOCK, BLOCK), pl.ds(c * BLOCK, BLOCK))
                wg[at] = wg[at] * (gate_mask[r, u * parts + c] > 0).astype(F32).astype(BF16)
                wu[at] = wu[at] * (up_mask[r, u * parts + c] > 0).astype(F32).astype(BF16)

    def prune_down():
        @pl.loop(0, chunks)
        def _(u):
            weight_copies(u)[2].wait()
            for r in range(side):
                for c in range(parts):
                    at = (u, pl.ds(c * BLOCK, BLOCK), pl.ds(r * BLOCK, BLOCK))
                    wd[at] = wd[at] * (down_mask[r, u * parts + c] > 0).astype(F32).astype(BF16)

    for step in range(1, n_col):
        cnt_copy(step).wait_recv()

    first, later = plan.sections
    p0, p1 = first // plan.n_dp, later // plan.n_dp
    counts = [cnt_all[shard][0:1, :] for shard in range(n_col)]

    def far(shard):
        return (shard - col) * (shard - col) * n_col + shard

    for shard in range(n_col):
        count = counts[shard]
        before = jnp.zeros((1, td), jnp.int32)
        for other in range(n_col):
            if other != shard:
                nearer = (far(other) < far(shard)).astype(jnp.int32)
                before = before + counts[other] * nearer
        cols = slice(shard * td, (shard + 1) * td)
        for path in range(2):
            for i, owner in enumerate(plan.orders[path]):
                target = 0
                for bit in range(k):
                    mine = bit_of(dp, bit)
                    target = target + (1 - mine if owner >> bit & 1 else mine) * (1 << bit)
                for into, size, base in ((place0, p0, 0), (place1, p1, first)):
                    lane = lax.broadcasted_iota(jnp.int32, (size, td), 1)
                    row = lax.broadcasted_iota(jnp.int32, (size, td), 0)
                    hit = (row + (target * size + base) - before == lane) & (lane < count)
                    ones = jnp.where(hit, 1.0, 0.0).astype(BF16)
                    into[path, i * size : (i + 1) * size, cols] = ones

    def compact(spots, buf):
        for path in range(2):
            total = None
            for shard in range(n_col):
                part = jnp.dot(
                    spots[path, :, shard * td : (shard + 1) * td],
                    buf[shard],
                    preferred_element_type=F32,
                )
                total = part if total is None else total + part
            yield path, total.astype(BF16)

    def compact_early():
        acc[...] = jnp.zeros_like(acc)
        for shard in range(n_col):

            @pl.when((shard - col <= plan.early) & (col - shard <= plan.early))
            def _():
                for path in range(2):
                    acc[pl.ds(path * first, first)] += jnp.dot(
                        place0[path, :, shard * td : (shard + 1) * td],
                        tok_all[shard],
                        preferred_element_type=F32,
                    )

        for path in range(2):
            tok0[path] = acc[pl.ds(path * first, first)].astype(BF16)

    class Scatter:
        def __init__(self, rows, keep, s0, r0, s1, r1, sem):
            self.rows, self.keep, self.bufs, self.sem = rows, keep, ((s0, r0), (s1, r1)), sem

        def copy(self, path, level, u):
            size = self.rows >> (level + 1)
            src, dst = self.bufs[min(level, 1)]
            start = 0 if level == 0 else (self.rows >> 1) - (self.rows >> level)
            at = (u, pl.ds(start, size))
            return remote(
                src.at[at], dst.at[at], self.sem, (level, u),
                dp=partner_of(dp, plan.bits[path][level]),
            )

        def put(self, path, u, value):
            half = self.rows >> 1
            src, _ = self.bufs[0]
            src[u] = value[half:].astype(BF16)
            self.keep[u] = value[:half]
            self.copy(path, 0, u).start()

        def got(self, path, level, u):
            copy = self.copy(path, level, u)
            copy.wait_recv()
            size = self.rows >> (level + 1)
            _, dst = self.bufs[min(level, 1)]
            start = 0 if level == 0 else (self.rows >> 1) - (self.rows >> level)
            return self.keep[u, 0:size] + dst[u, pl.ds(start, size)].astype(F32)

        def step(self, path, level, u):
            value = self.got(path, level - 1, u)
            size = self.rows >> (level + 1)
            start = (self.rows >> 1) - (self.rows >> level)
            src, _ = self.bufs[1]
            src[u, pl.ds(start, size)] = value[size:].astype(BF16)
            self.keep[u, 0:size] = value[:size]
            self.copy(path, level, u).start()

    gu0 = Scatter(first, keep0, s00, r00, s10, r10, gu0_sem)
    gu1 = Scatter(later, keep1, s01, r01, s11, r11, gu1_sem)
    bk = Scatter(rows, bkeep, bs0, br0, bs1, br1, bk_sem)

    def gather_copy(buf, sem, path, level, u):
        size = rows >> (level + 1)
        return remote(
            buf.at[u, pl.ds(0, size)], buf.at[u, pl.ds(size, size)], sem, (level, u),
            dp=partner_of(dp, plan.bits[path][level]),
        )

    def gate_up(left, gu, u, path):
        value = jnp.concatenate(
            [
                jnp.dot(left[path], wg[u], preferred_element_type=F32),
                jnp.dot(left[path], wu[u], preferred_element_type=F32),
            ],
            axis=1,
        )
        gu.put(path, u, value)

    def early_part(lo, hi):
        @pl.loop(lo, hi)
        def _(j):
            for path in range(2):
                u = path * per + j
                prune_in(u)
                gate_up(tok0, gu0, u, path)

            @pl.when(j >= 1)
            def _():
                for path in range(2):
                    gu0.step(path, 1, path * per + j - 1)

    def hop_next(step):
        hop_wait_recv(tok_bufs, step)
        if step + 1 < n_col - 1:
            hop_start(tok_bufs, step + 1)
        else:
            hop_start(cot_bufs, 0)

    for step in range(plan.early):
        hop_next(step)
    compact_early()
    early_part(0, per // 2)
    if plan.early < n_col - 1:
        hop_next(plan.early)
    early_part(per // 2, per)
    for step in range(plan.early + 1, n_col - 1):
        hop_next(step)
    for path in range(2):
        gu0.step(path, 1, path * per + per - 1)
    for path, value in compact(place1, tok_all):
        tok1[path] = value

    @pl.loop(0, per)
    def _(j):
        for path in range(2):
            gate_up(tok1, gu1, path * per + j, path)

        @pl.when(j >= 1)
        def _():
            for path in range(2):
                gu1.step(path, 1, path * per + j - 1)

        if k > 2:
            for path in range(2):
                gu0.step(path, 2, path * per + j)

    for path in range(2):
        gu1.step(path, 1, path * per + per - 1)

    def tok_copies(path, i):
        return [
            pltpu.make_async_copy(
                src.at[path, pl.ds(i * size, size)],
                tokc.at[path, pl.ds(i * piece + off, size)],
                tok_sem.at[path, i, n],
            )
            for n, (src, size, off) in enumerate(((tok0, p0, 0), (tok1, p1, p0)))
        ]

    for path in range(2):
        for i in range(plan.n_dp):
            for copy in tok_copies(path, i):
                copy.start()

    prune_down()

    for step in range(1, n_col - 1):
        hop_wait_recv(cot_bufs, step - 1)
        hop_start(cot_bufs, step)
    if k > 2:

        @pl.loop(0, per)
        def _(j):
            for path in range(2):
                gu1.step(path, 2, path * per + j)

    hop_wait_recv(cot_bufs, n_col - 2)
    for spots, size, off in ((place0, p0, 0), (place1, p1, p0)):
        for path, value in compact(spots, cot_all):
            for i in range(plan.n_dp):
                at = i * piece + off
                gc[path, at : at + size] = value[i * size : (i + 1) * size]

    @pl.loop(0, per)
    def _(j):
        for path in range(2):
            u = path * per + j
            value = lax.dot_general(
                gc[path], wd[u], (((1,), (1,)), ((), ())), preferred_element_type=F32
            )
            bk.put(path, u, value)

        @pl.when(j >= 1)
        def _():
            for path in range(2):
                bk.step(path, 1, path * per + j - 1)

    for path in range(2):
        bk.step(path, 1, path * per + per - 1)

    for level in range(3, k):

        @pl.loop(0, per)
        def _(j):
            for path in range(2):
                gu0.step(path, level, path * per + j)
                gu1.step(path, level, path * per + j)

    @pl.loop(0, per)
    def _(j):
        for path in range(2):
            u = path * per + j
            value0, value1 = gu0.got(path, k - 1, u), gu1.got(path, k - 1, u)
            keep0[u, 0:p0] = value0
            keep1[u, 0:p1] = value1
            value = jnp.concatenate([value0, value1], axis=0)
            gate, upward = value[:, :wide], value[:, wide:]
            sigma = 1.0 / (1.0 + jnp.exp(-gate))
            hid[u, 0:piece] = (gate * sigma * upward).astype(BF16)
            gather_copy(hid, hid_sem, path, k - 1, u).start()

    def gather_step(buf, sem, level):
        @pl.loop(0, per)
        def _(j):
            for path in range(2):
                u = path * per + j
                gather_copy(buf, sem, path, level + 1, u).wait_recv()
                gather_copy(buf, sem, path, level, u).start()

    gather_step(hid, hid_sem, k - 2)

    for level in range(2, k):

        @pl.loop(0, per)
        def _(j):
            for path in range(2):
                bk.step(path, level, path * per + j)

    for level in range(k - 3, -1, -1):
        gather_step(hid, hid_sem, level)

    @pl.loop(0, per)
    def _(j):
        for path in range(2):
            u = path * per + j
            back = bk.got(path, k - 1, u)
            value = jnp.concatenate([keep0[u, 0:p0], keep1[u, 0:p1]], axis=0)
            gate, upward = value[:, :wide], value[:, wide:]
            sigma = 1.0 / (1.0 + jnp.exp(-gate))
            dd[u, 0:piece, 0:wide] = (
                back * upward * sigma * (1.0 + gate * (1.0 - sigma))
            ).astype(BF16)
            dd[u, 0:piece, wide : 2 * wide] = (back * (gate * sigma)).astype(BF16)
            gather_copy(dd, d_sem, path, k - 1, u).start()

    acc[...] = jnp.zeros_like(acc)

    @pl.loop(0, per)
    def _(j):
        for path in range(2):
            u = path * per + j
            gather_copy(hid, hid_sem, path, 0, u).wait_recv()
            left = hid[u]
            if path == 1:
                spots = [plan.orders[1].index(owner) * piece for owner in plan.orders[0]]
                left = jnp.concatenate([left[at : at + piece] for at in spots], axis=0)
            acc[0:rows] += jnp.dot(left, wd[u], preferred_element_type=F32)

    mixed = acc[0:rows].astype(BF16)
    mixes = [
        jnp.concatenate([mixed[at : at + size] for at in range(off, rows, piece)], axis=0)
        for size, off in ((p0, 0), (p1, p0))
    ]
    for shard in range(n_col):
        total = None
        for spots, mix in zip((place0, place1), mixes):
            part = lax.dot_general(
                spots[0, :, shard * td : (shard + 1) * td],
                mix,
                (((0,), (0,)), ((), ())),
                preferred_element_type=F32,
            )
            total = part if total is None else total + part
        zs[shard] = total.astype(BF16)

    def z_copy(step):
        to = (col + step) % n_col
        return remote(zs.at[to], zr.at[step - 1], z_sem, (step - 1,), col=to)

    for step in range(1, n_col):
        z_copy(step).start()

    gather_step(dd, d_sem, k - 2)

    def down_copy(path, u):
        return pltpu.make_async_copy(
            down.at[path],
            down_out.at[pl.ds(pl.multiple_of(u * wide, wide), wide), :],
            out_sem.at[0, path],
        )

    @pl.loop(0, per)
    def _(j):
        for path in range(2):
            u = path * per + j

            @pl.when(j >= 1)
            def _():
                down_copy(path, u - 1).wait()

            down[path] = lax.dot_general(
                hid[u], gc[path], (((0,), (0,)), ((), ())), preferred_element_type=F32
            ).astype(BF16)
            down_copy(path, u).start()

    for level in range(k - 3, -1, -1):
        gather_step(dd, d_sem, level)

    @pl.loop(0, per)
    def _(j):
        for path in range(2):
            u = path * per + j
            gather_copy(dd, d_sem, path, 0, u).wait_recv()
            pltpu.make_async_copy(dd.at[u], d_out.at[u], out_sem.at[1, u]).start()

    total = zs[col].astype(F32)
    for step in range(1, n_col):
        z_copy(step).wait_recv()
        total = total + zr[step - 1].astype(F32)
    out_ref[...] = total.astype(BF16)

    for step in range(1, n_col):
        z_copy(step).wait_send()
    for step in range(n_col - 1):
        cnt_copy(step + 1).wait_send()
        hop_wait_send(tok_bufs, step)
        hop_wait_send(cot_bufs, step)

    for path in range(2):
        down_copy(path, path * per + per - 1).wait()
        for i in range(plan.n_dp):
            for copy in tok_copies(path, i):
                copy.wait()

    @pl.loop(0, per)
    def _(j):
        for path in range(2):
            u = path * per + j
            for level in range(k):
                gu0.copy(path, level, u).wait_send()
                gu1.copy(path, level, u).wait_send()
                bk.copy(path, level, u).wait_send()
                gather_copy(hid, hid_sem, path, level, u).wait_send()
                gather_copy(dd, d_sem, path, level, u).wait_send()
            pltpu.make_async_copy(dd.at[u], d_out.at[u], out_sem.at[1, u]).wait()


def exchange(plan, cnt, tokens, cotangent, gate_mask, up_mask, down_mask, wg, wu, wd):
    n_col, k, td, wide = plan.n_col, plan.levels, plan.tok_dev, plan.wide
    rows, chunks, feats = plan.rows, plan.chunks, plan.feats
    first, later = plan.sections
    vmem, smem = pl.BlockSpec(memory_space=pltpu.VMEM), pl.BlockSpec(memory_space=pltpu.SMEM)
    whole = pl.BlockSpec(memory_space=pl.ANY)

    def scatter_bufs(rows, width):
        half = rows // 2
        rest = half - (rows >> k)
        return [
            pltpu.VMEM((chunks, half, width), F32),
            pltpu.VMEM((chunks, half, width), BF16),
            pltpu.VMEM((chunks, half, width), BF16),
            pltpu.VMEM((chunks, rest, width), BF16),
            pltpu.VMEM((chunks, rest, width), BF16),
        ]

    return pl.pallas_call(
        functools.partial(exchange_kernel, plan),
        out_shape=(
            jax.ShapeDtypeStruct((td, feats), BF16),
            jax.ShapeDtypeStruct((2, rows, feats), BF16),
            jax.ShapeDtypeStruct((chunks, rows, 2 * wide), BF16),
            jax.ShapeDtypeStruct((plan.units, feats), BF16),
        ),
        in_specs=[vmem, vmem, vmem, smem, smem, smem, whole, whole, whole],
        out_specs=(vmem, whole, whole, whole),
        scratch_shapes=[
            pltpu.VMEM((n_col, 8, 128), jnp.int32),
            pltpu.VMEM((n_col, td, feats), BF16),
            pltpu.VMEM((n_col, td, feats), BF16),
            pltpu.VMEM((2, rows, feats), BF16),
            pltpu.VMEM((2, first, n_col * td), BF16),
            pltpu.VMEM((2, later, n_col * td), BF16),
            pltpu.VMEM((2, first, feats), BF16),
            pltpu.VMEM((2, later, feats), BF16),
            pltpu.VMEM((chunks, feats, wide), BF16),
            pltpu.VMEM((chunks, feats, wide), BF16),
            pltpu.VMEM((chunks, wide, feats), BF16),
            pltpu.SemaphoreType.DMA((3, chunks)),
            *scatter_bufs(first, 2 * wide),
            *scatter_bufs(later, 2 * wide),
            *scatter_bufs(rows, wide),
            pltpu.VMEM((chunks, rows, wide), BF16),
            pltpu.VMEM((chunks, rows, 2 * wide), BF16),
            pltpu.VMEM((max(rows, 2 * first), feats), F32),
            pltpu.VMEM((n_col, td, feats), BF16),
            pltpu.VMEM((n_col - 1, td, feats), BF16),
            pltpu.VMEM((2, wide, feats), BF16),
            pltpu.SemaphoreType.DMA((2, n_col - 1)),
            pltpu.SemaphoreType.DMA((2, 2, 2, n_col - 1)),
            pltpu.SemaphoreType.DMA((2, k, chunks)),
            pltpu.SemaphoreType.DMA((2, k, chunks)),
            pltpu.SemaphoreType.DMA((2, k, chunks)),
            pltpu.SemaphoreType.DMA((2, k, chunks)),
            pltpu.SemaphoreType.DMA((2, k, chunks)),
            pltpu.SemaphoreType.DMA((2, n_col - 1)),
            pltpu.SemaphoreType.DMA((2, chunks)),
            pltpu.SemaphoreType.DMA((2, plan.n_dp, 2)),
        ],
        compiler_params=pltpu.CompilerParams(
            collective_id=0, has_side_effects=True, vmem_limit_bytes=63 * 2**20
        ),
    )(cnt, tokens, cotangent, gate_mask, up_mask, down_mask, wg, wu, wd)


def grads_kernel(
    plan, gate_mask, up_mask, down_mask, tokc, dd, down, gate_grad, up_grad, down_grad, turned
):
    u = pl.program_id(0)
    wide = plan.wide
    side, parts = plan.feats // BLOCK, wide // BLOCK

    @pl.when((u == 0) | (u == plan.per_path))
    def _():
        turned[...] = tokc[0].T

    def keep(mask, value):
        return jnp.where(mask > 0, value, 0.0)

    for ref, mask, lo in ((gate_grad, gate_mask, 0), (up_grad, up_mask, wide)):
        value = jnp.dot(turned[...], dd[0, :, lo : lo + wide], preferred_element_type=F32)
        for r in range(side):
            for c in range(parts):
                rs, cs = slice(r * BLOCK, (r + 1) * BLOCK), slice(c * BLOCK, (c + 1) * BLOCK)
                ref[rs, cs] = keep(mask[r, u * parts + c], value[rs, cs])
    for r in range(side):
        for c in range(parts):
            rs, cs = slice(r * BLOCK, (r + 1) * BLOCK), slice(c * BLOCK, (c + 1) * BLOCK)
            down_grad[cs, rs] = keep(down_mask[r, u * parts + c], down[cs, rs].astype(F32))


def grads(plan, gate_mask, up_mask, down_mask, tokc, dd, down):
    rows, feats, wide, per = plan.rows, plan.feats, plan.wide, plan.per_path
    smem = pl.BlockSpec(memory_space=pltpu.SMEM)
    return pl.pallas_call(
        functools.partial(grads_kernel, plan),
        grid=(plan.chunks,),
        out_shape=(
            jax.ShapeDtypeStruct((feats, plan.units), F32),
            jax.ShapeDtypeStruct((feats, plan.units), F32),
            jax.ShapeDtypeStruct((plan.units, feats), F32),
        ),
        in_specs=[
            smem,
            smem,
            smem,
            pl.BlockSpec((1, rows, feats), lambda u: (u // per, 0, 0)),
            pl.BlockSpec((1, rows, 2 * wide), lambda u: (u, 0, 0)),
            pl.BlockSpec((wide, feats), lambda u: (u, 0)),
        ],
        out_specs=(
            pl.BlockSpec((feats, wide), lambda u: (0, u)),
            pl.BlockSpec((feats, wide), lambda u: (0, u)),
            pl.BlockSpec((wide, feats), lambda u: (u, 0)),
        ),
        scratch_shapes=[pltpu.VMEM((feats, rows), BF16)],
        compiler_params=pltpu.CompilerParams(vmem_limit_bytes=63 * 2**20),
    )(gate_mask, up_mask, down_mask, tokc, dd, down)


def on_device(
    n_col, n_dp,
    tokens, cotangent, gate_weight, up_weight, down_weight, gate_mask, up_mask, down_mask, counts
):
    plan = Plan(n_col, n_dp, tokens.shape[0], tokens.shape[1], gate_weight.shape[1])
    cnt = jnp.broadcast_to(counts.reshape(1, 1), (8, 128))
    down_mask = down_mask.T
    output, tokc, dd, down = exchange(
        plan, cnt, tokens, cotangent, gate_mask, up_mask, down_mask,
        gate_weight, up_weight, down_weight,
    )
    gate_grad, up_grad, down_grad = grads(plan, gate_mask, up_mask, down_mask, tokc, dd, down)
    return (output, gate_grad, up_grad, down_grad)


def solution(mesh):
    in_specs = (
        P("col", "dp"),
        P("col", "dp"),
        P("dp", "col"),
        P("dp", "col"),
        P("col", "dp"),
        P("dp", "col"),
        P("dp", "col"),
        P("col", "dp"),
        P("col"),
    )
    out_specs = (P("col", "dp"), P("dp", "col"), P("dp", "col"), P("col", "dp"))
    return jax.shard_map(
        functools.partial(on_device, mesh.shape["col"], mesh.shape["dp"]),
        mesh=mesh,
        in_specs=in_specs,
        out_specs=out_specs,
        check_vma=False,
    )
```

```python
import functools

import jax
import jax.numpy as jnp
from jax import lax
from jax.experimental import pallas as pl
from jax.experimental.pallas import tpu as pltpu
from jax.sharding import PartitionSpec as P

MESH = pl.DeviceIdType.MESH
BLOCK = 128
F32 = jnp.float32
BF16 = jnp.bfloat16


class Plan:
    def __init__(self, n_col, n_dp, tok_dev, feats, units):
        self.n_col, self.n_dp, self.tok_dev, self.feats, self.units = n_col, n_dp, tok_dev, feats, units
        self.levels = n_dp.bit_length() - 1
        self.rows = n_col * tok_dev * 3 // 4
        self.piece = self.rows // n_dp
        half = units // 2
        self.wide = 256 if half % 256 == 0 else BLOCK
        self.per_path = half // self.wide
        self.chunks = 2 * self.per_path
        k = self.levels
        self.bits = [list(range(k)), [0] + list(range(k - 1, 0, -1))]
        first, dead = 16 * n_dp, n_col * tok_dev - self.rows
        self.early = -(-(first + dead) // tok_dev) - 1
        self.sections = [first, self.rows - first]
        self.orders = []
        for bits in self.bits:
            order = []
            for place in range(n_dp):
                owner = 0
                for level, bit in enumerate(bits):
                    if place >> (k - 1 - level) & 1:
                        owner |= 1 << bit
                order.append(owner)
            self.orders.append(order)


def bit_of(index, bit):
    return (index // (1 << bit)) % 2


def partner_of(index, bit):
    return index + (1 - 2 * bit_of(index, bit)) * (1 << bit)


def exchange_kernel(
    plan,
    cnt_ref, tok_ref, cot_ref, gate_mask, up_mask, down_mask, wg_hbm, wu_hbm, wd_hbm,
    out_ref, tokc, gc, hid_out, d_out,
    cnt_all, tok_all, cot_all, place0, place1, tok0, tok1, wg, wu, wd, w_sem,
    keep0, s00, r00, s10, r10, keep1, s01, r01, s11, r11, bkeep, bs0, br0, bs1, br1,
    hid, dd, acc, zs, zr,
    cnt_sem, ring_sem, gu0_sem, gu1_sem, bk_sem, hid_sem, d_sem, z_sem, out_sem, tok_sem,
):
    n_col, k, td, wide = plan.n_col, plan.levels, plan.tok_dev, plan.wide
    rows, piece, per, chunks = plan.rows, plan.piece, plan.per_path, plan.chunks
    col, dp = lax.axis_index("col"), lax.axis_index("dp")

    def remote(src, dst, sems, at, **to):
        return pltpu.make_async_remote_copy(
            src_ref=src,
            dst_ref=dst,
            send_sem=sems.at[(0, *at)],
            recv_sem=sems.at[(1, *at)],
            device_id=(to.get("col", col), to.get("dp", dp)),
            device_id_type=MESH,
        )

    def weight_copies(u):
        cols = pl.ds(pl.multiple_of(u * wide, wide), wide)
        return (
            pltpu.make_async_copy(wg_hbm.at[:, cols], wg.at[u], w_sem.at[0, u]),
            pltpu.make_async_copy(wu_hbm.at[:, cols], wu.at[u], w_sem.at[1, u]),
            pltpu.make_async_copy(wd_hbm.at[cols, :], wd.at[u], w_sem.at[2, u]),
        )

    @pl.loop(0, chunks)
    def _(u):
        for copy in weight_copies(u)[:2]:
            copy.start()

    @pl.loop(0, chunks)
    def _(u):
        weight_copies(u)[2].start()

    barrier = pltpu.get_barrier_semaphore()
    for bit in range(k):
        pl.semaphore_signal(
            barrier, inc=1, device_id=(col, partner_of(dp, bit)), device_id_type=MESH
        )
    for step in range(1, n_col):
        pl.semaphore_signal(
            barrier, inc=1, device_id=((col + step) % n_col, dp), device_id_type=MESH
        )
    pl.semaphore_wait(barrier, k + n_col - 1)

    cnt_all[col] = cnt_ref[...]
    tok_all[col] = tok_ref[...]
    live = lax.broadcasted_iota(jnp.int32, (td, plan.feats), 0) < cnt_ref[0:1, 0:1]
    cot_all[col] = jnp.where(live, cot_ref[...].astype(F32), 0.0).astype(BF16)

    def hop(bufs, way, step, name):
        first, last = bufs
        block = col - step if way == 0 else col + step
        to = col + 1 if way == 0 else col - 1
        return [
            remote(buf.at[block], buf.at[block], ring_sem, (first + i, way, step), col=to)
            for i, buf in enumerate(last)
        ]

    def sends(way, step):
        return (
            (col - step >= 0) & (col + 1 < n_col) if way == 0 else (col + step < n_col) & (col >= 1)
        )

    def receives(way, step):
        return col - 1 - step >= 0 if way == 0 else col + 1 + step < n_col

    def hop_start(bufs, step):
        for way in range(2):

            @pl.when(sends(way, step))
            def _():
                for copy in hop(bufs, way, step, "s"):
                    copy.start()

    def hop_wait_recv(bufs, step):
        for way in range(2):

            @pl.when(receives(way, step))
            def _():
                first, last = bufs
                block = col - 1 - step if way == 0 else col + 1 + step
                for i, buf in enumerate(last):
                    remote(
                        buf.at[block], buf.at[block], ring_sem, (first + i, way, step), col=block
                    ).wait_recv()

    def hop_wait_send(bufs, step):
        for way in range(2):

            @pl.when(sends(way, step))
            def _():
                for copy in hop(bufs, way, step, "w"):
                    copy.wait_send()

    def cnt_copy(step):
        to = (col + step) % n_col
        return remote(cnt_all.at[col], cnt_all.at[col], cnt_sem, (step - 1,), col=to)

    for step in range(1, n_col):
        cnt_copy(step).start()
    tok_bufs = (0, [tok_all])
    cot_bufs = (1, [cot_all])
    hop_start(tok_bufs, 0)

    side, parts = plan.feats // BLOCK, wide // BLOCK

    def prune_in(u):
        for copy in weight_copies(u)[:2]:
            copy.wait()
        for r in range(side):
            for c in range(parts):
                at = (u, pl.ds(r * BLOCK, BLOCK), pl.ds(c * BLOCK, BLOCK))
                wg[at] = wg[at] * (gate_mask[r, u * parts + c] > 0).astype(F32).astype(BF16)
                wu[at] = wu[at] * (up_mask[r, u * parts + c] > 0).astype(F32).astype(BF16)

    def prune_down():
        @pl.loop(0, chunks)
        def _(u):
            weight_copies(u)[2].wait()
            for r in range(side):
                for c in range(parts):
                    at = (u, pl.ds(c * BLOCK, BLOCK), pl.ds(r * BLOCK, BLOCK))
                    wd[at] = wd[at] * (down_mask[r, u * parts + c] > 0).astype(F32).astype(BF16)

    for step in range(1, n_col):
        cnt_copy(step).wait_recv()

    first, later = plan.sections
    p0, p1 = first // plan.n_dp, later // plan.n_dp
    counts = [cnt_all[shard][0:1, :] for shard in range(n_col)]

    def far(shard):
        return (shard - col) * (shard - col) * n_col + shard

    for shard in range(n_col):
        count = counts[shard]
        before = jnp.zeros((1, td), jnp.int32)
        for other in range(n_col):
            if other != shard:
                nearer = (far(other) < far(shard)).astype(jnp.int32)
                before = before + counts[other] * nearer
        cols = slice(shard * td, (shard + 1) * td)
        for path in range(2):
            for i, owner in enumerate(plan.orders[path]):
                target = 0
                for bit in range(k):
                    mine = bit_of(dp, bit)
                    target = target + (1 - mine if owner >> bit & 1 else mine) * (1 << bit)
                for into, size, base in ((place0, p0, 0), (place1, p1, first)):
                    lane = lax.broadcasted_iota(jnp.int32, (size, td), 1)
                    row = lax.broadcasted_iota(jnp.int32, (size, td), 0)
                    hit = (row + (target * size + base) - before == lane) & (lane < count)
                    ones = jnp.where(hit, 1.0, 0.0).astype(BF16)
                    into[path, i * size : (i + 1) * size, cols] = ones

    def compact(spots, buf):
        for path in range(2):
            total = None
            for shard in range(n_col):
                part = jnp.dot(
                    spots[path, :, shard * td : (shard + 1) * td],
                    buf[shard],
                    preferred_element_type=F32,
                )
                total = part if total is None else total + part
            yield path, total.astype(BF16)

    def compact_early():
        acc[...] = jnp.zeros_like(acc)
        for shard in range(n_col):

            @pl.when((shard - col <= plan.early) & (col - shard <= plan.early))
            def _():
                for path in range(2):
                    acc[pl.ds(path * first, first)] += jnp.dot(
                        place0[path, :, shard * td : (shard + 1) * td],
                        tok_all[shard],
                        preferred_element_type=F32,
                    )

        for path in range(2):
            tok0[path] = acc[pl.ds(path * first, first)].astype(BF16)

    class Scatter:
        def __init__(self, rows, keep, s0, r0, s1, r1, sem):
            self.rows, self.keep, self.bufs, self.sem = rows, keep, ((s0, r0), (s1, r1)), sem

        def copy(self, path, level, u):
            size = self.rows >> (level + 1)
            src, dst = self.bufs[min(level, 1)]
            start = 0 if level == 0 else (self.rows >> 1) - (self.rows >> level)
            at = (u, pl.ds(start, size))
            return remote(
                src.at[at], dst.at[at], self.sem, (level, u),
                dp=partner_of(dp, plan.bits[path][level]),
            )

        def put(self, path, u, value):
            half = self.rows >> 1
            src, _ = self.bufs[0]
            src[u] = value[half:].astype(BF16)
            self.keep[u] = value[:half]
            self.copy(path, 0, u).start()

        def got(self, path, level, u):
            copy = self.copy(path, level, u)
            copy.wait_recv()
            size = self.rows >> (level + 1)
            _, dst = self.bufs[min(level, 1)]
            start = 0 if level == 0 else (self.rows >> 1) - (self.rows >> level)
            return self.keep[u, 0:size] + dst[u, pl.ds(start, size)].astype(F32)

        def step(self, path, level, u):
            value = self.got(path, level - 1, u)
            size = self.rows >> (level + 1)
            start = (self.rows >> 1) - (self.rows >> level)
            src, _ = self.bufs[1]
            src[u, pl.ds(start, size)] = value[size:].astype(BF16)
            self.keep[u, 0:size] = value[:size]
            self.copy(path, level, u).start()

    gu0 = Scatter(first, keep0, s00, r00, s10, r10, gu0_sem)
    gu1 = Scatter(later, keep1, s01, r01, s11, r11, gu1_sem)
    bk = Scatter(rows, bkeep, bs0, br0, bs1, br1, bk_sem)

    def gather_copy(buf, sem, path, level, u):
        size = rows >> (level + 1)
        return remote(
            buf.at[u, pl.ds(0, size)], buf.at[u, pl.ds(size, size)], sem, (level, u),
            dp=partner_of(dp, plan.bits[path][level]),
        )

    def gate_up(left, gu, u, path):
        value = jnp.concatenate(
            [
                jnp.dot(left[path], wg[u], preferred_element_type=F32),
                jnp.dot(left[path], wu[u], preferred_element_type=F32),
            ],
            axis=1,
        )
        gu.put(path, u, value)

    def early_part(lo, hi):
        @pl.loop(lo, hi)
        def _(j):
            for path in range(2):
                u = path * per + j
                prune_in(u)
                gate_up(tok0, gu0, u, path)

            @pl.when(j >= 1)
            def _():
                for path in range(2):
                    gu0.step(path, 1, path * per + j - 1)

    def hop_next(step):
        hop_wait_recv(tok_bufs, step)
        if step + 1 < n_col - 1:
            hop_start(tok_bufs, step + 1)
        else:
            hop_start(cot_bufs, 0)

    for step in range(plan.early):
        hop_next(step)
    compact_early()
    early_part(0, per // 2)
    if plan.early < n_col - 1:
        hop_next(plan.early)
    early_part(per // 2, per)
    for step in range(plan.early + 1, n_col - 1):
        hop_next(step)
    for path in range(2):
        gu0.step(path, 1, path * per + per - 1)
    for path, value in compact(place1, tok_all):
        tok1[path] = value

    @pl.loop(0, per)
    def _(j):
        for path in range(2):
            gate_up(tok1, gu1, path * per + j, path)

        @pl.when(j >= 1)
        def _():
            for path in range(2):
                gu1.step(path, 1, path * per + j - 1)

        if k > 2:
            for path in range(2):
                gu0.step(path, 2, path * per + j)

    for path in range(2):
        gu1.step(path, 1, path * per + per - 1)

    def tok_copies(path, i):
        return [
            pltpu.make_async_copy(
                src.at[path, pl.ds(i * size, size)],
                tokc.at[path, pl.ds(i * piece + off, size)],
                tok_sem.at[path, i, n],
            )
            for n, (src, size, off) in enumerate(((tok0, p0, 0), (tok1, p1, p0)))
        ]

    for path in range(2):
        for i in range(plan.n_dp):
            for copy in tok_copies(path, i):
                copy.start()

    prune_down()

    for step in range(1, n_col - 1):
        hop_wait_recv(cot_bufs, step - 1)
        hop_start(cot_bufs, step)
    if k > 2:

        @pl.loop(0, per)
        def _(j):
            for path in range(2):
                gu1.step(path, 2, path * per + j)

    hop_wait_recv(cot_bufs, n_col - 2)
    for spots, size, off in ((place0, p0, 0), (place1, p1, p0)):
        for path, value in compact(spots, cot_all):
            for i in range(plan.n_dp):
                at = i * piece + off
                gc[path, at : at + size] = value[i * size : (i + 1) * size]

    @pl.loop(0, per)
    def _(j):
        for path in range(2):
            u = path * per + j
            value = lax.dot_general(
                gc[path], wd[u], (((1,), (1,)), ((), ())), preferred_element_type=F32
            )
            bk.put(path, u, value)

        @pl.when(j >= 1)
        def _():
            for path in range(2):
                bk.step(path, 1, path * per + j - 1)

    for path in range(2):
        bk.step(path, 1, path * per + per - 1)

    for level in range(3, k):

        @pl.loop(0, per)
        def _(j):
            for path in range(2):
                gu0.step(path, level, path * per + j)
                gu1.step(path, level, path * per + j)

    @pl.loop(0, per)
    def _(j):
        for path in range(2):
            u = path * per + j
            value0, value1 = gu0.got(path, k - 1, u), gu1.got(path, k - 1, u)
            keep0[u, 0:p0] = value0
            keep1[u, 0:p1] = value1
            value = jnp.concatenate([value0, value1], axis=0)
            gate, upward = value[:, :wide], value[:, wide:]
            sigma = 1.0 / (1.0 + jnp.exp(-gate))
            hid[u, 0:piece] = (gate * sigma * upward).astype(BF16)
            gather_copy(hid, hid_sem, path, k - 1, u).start()

    def gather_step(buf, sem, level):
        @pl.loop(0, per)
        def _(j):
            for path in range(2):
                u = path * per + j
                gather_copy(buf, sem, path, level + 1, u).wait_recv()
                gather_copy(buf, sem, path, level, u).start()

    gather_step(hid, hid_sem, k - 2)

    for level in range(2, k):

        @pl.loop(0, per)
        def _(j):
            for path in range(2):
                bk.step(path, level, path * per + j)

    for level in range(k - 3, -1, -1):
        gather_step(hid, hid_sem, level)

    @pl.loop(0, per)
    def _(j):
        for path in range(2):
            u = path * per + j
            back = bk.got(path, k - 1, u)
            value = jnp.concatenate([keep0[u, 0:p0], keep1[u, 0:p1]], axis=0)
            gate, upward = value[:, :wide], value[:, wide:]
            sigma = 1.0 / (1.0 + jnp.exp(-gate))
            dd[u, 0:piece, 0:wide] = (
                back * upward * sigma * (1.0 + gate * (1.0 - sigma))
            ).astype(BF16)
            dd[u, 0:piece, wide : 2 * wide] = (back * (gate * sigma)).astype(BF16)
            gather_copy(dd, d_sem, path, k - 1, u).start()

    acc[...] = jnp.zeros_like(acc)

    @pl.loop(0, per)
    def _(j):
        for path in range(2):
            u = path * per + j
            gather_copy(dd, d_sem, path, k - 1, u).wait_recv()
            gather_copy(dd, d_sem, path, k - 2, u).start()
            gather_copy(hid, hid_sem, path, 0, u).wait_recv()
            pltpu.make_async_copy(hid.at[u], hid_out.at[u], out_sem.at[0, u]).start()
            left = hid[u]
            if path == 1:
                spots = [plan.orders[1].index(owner) * piece for owner in plan.orders[0]]
                left = jnp.concatenate([left[at : at + piece] for at in spots], axis=0)
            acc[0:rows] += jnp.dot(left, wd[u], preferred_element_type=F32)

    mixed = acc[0:rows].astype(BF16)
    mixes = [
        jnp.concatenate([mixed[at : at + size] for at in range(off, rows, piece)], axis=0)
        for size, off in ((p0, 0), (p1, p0))
    ]
    for shard in range(n_col):
        total = None
        for spots, mix in zip((place0, place1), mixes):
            part = lax.dot_general(
                spots[0, :, shard * td : (shard + 1) * td],
                mix,
                (((0,), (0,)), ((), ())),
                preferred_element_type=F32,
            )
            total = part if total is None else total + part
        zs[shard] = total.astype(BF16)

    def z_copy(step):
        to = (col + step) % n_col
        return remote(zs.at[to], zr.at[step - 1], z_sem, (step - 1,), col=to)

    for step in range(1, n_col):
        z_copy(step).start()

    for level in range(k - 3, -1, -1):
        gather_step(dd, d_sem, level)

    @pl.loop(0, per)
    def _(j):
        for path in range(2):
            u = path * per + j
            gather_copy(dd, d_sem, path, 0, u).wait_recv()
            pltpu.make_async_copy(dd.at[u], d_out.at[u], out_sem.at[1, u]).start()

    total = zs[col].astype(F32)
    for step in range(1, n_col):
        z_copy(step).wait_recv()
        total = total + zr[step - 1].astype(F32)
    out_ref[...] = total.astype(BF16)

    for step in range(1, n_col):
        z_copy(step).wait_send()
    for step in range(n_col - 1):
        cnt_copy(step + 1).wait_send()
        hop_wait_send(tok_bufs, step)
        hop_wait_send(cot_bufs, step)

    for path in range(2):
        for i in range(plan.n_dp):
            for copy in tok_copies(path, i):
                copy.wait()

    @pl.loop(0, per)
    def _(j):
        for path in range(2):
            u = path * per + j
            for level in range(k):
                gu0.copy(path, level, u).wait_send()
                gu1.copy(path, level, u).wait_send()
                bk.copy(path, level, u).wait_send()
                gather_copy(hid, hid_sem, path, level, u).wait_send()
                gather_copy(dd, d_sem, path, level, u).wait_send()
            pltpu.make_async_copy(hid.at[u], hid_out.at[u], out_sem.at[0, u]).wait()
            pltpu.make_async_copy(dd.at[u], d_out.at[u], out_sem.at[1, u]).wait()


def exchange(plan, cnt, tokens, cotangent, gate_mask, up_mask, down_mask, wg, wu, wd):
    n_col, k, td, wide = plan.n_col, plan.levels, plan.tok_dev, plan.wide
    rows, chunks, feats = plan.rows, plan.chunks, plan.feats
    first, later = plan.sections
    vmem, smem = pl.BlockSpec(memory_space=pltpu.VMEM), pl.BlockSpec(memory_space=pltpu.SMEM)
    whole = pl.BlockSpec(memory_space=pl.ANY)

    def scatter_bufs(rows, width):
        half = rows // 2
        rest = half - (rows >> k)
        return [
            pltpu.VMEM((chunks, half, width), F32),
            pltpu.VMEM((chunks, half, width), BF16),
            pltpu.VMEM((chunks, half, width), BF16),
            pltpu.VMEM((chunks, rest, width), BF16),
            pltpu.VMEM((chunks, rest, width), BF16),
        ]

    return pl.pallas_call(
        functools.partial(exchange_kernel, plan),
        out_shape=(
            jax.ShapeDtypeStruct((td, feats), BF16),
            jax.ShapeDtypeStruct((2, rows, feats), BF16),
            jax.ShapeDtypeStruct((2, rows, feats), BF16),
            jax.ShapeDtypeStruct((chunks, rows, wide), BF16),
            jax.ShapeDtypeStruct((chunks, rows, 2 * wide), BF16),
        ),
        in_specs=[vmem, vmem, vmem, smem, smem, smem, whole, whole, whole],
        out_specs=(vmem, whole, vmem, whole, whole),
        scratch_shapes=[
            pltpu.VMEM((n_col, 8, 128), jnp.int32),
            pltpu.VMEM((n_col, td, feats), BF16),
            pltpu.VMEM((n_col, td, feats), BF16),
            pltpu.VMEM((2, first, n_col * td), BF16),
            pltpu.VMEM((2, later, n_col * td), BF16),
            pltpu.VMEM((2, first, feats), BF16),
            pltpu.VMEM((2, later, feats), BF16),
            pltpu.VMEM((chunks, feats, wide), BF16),
            pltpu.VMEM((chunks, feats, wide), BF16),
            pltpu.VMEM((chunks, wide, feats), BF16),
            pltpu.SemaphoreType.DMA((3, chunks)),
            *scatter_bufs(first, 2 * wide),
            *scatter_bufs(later, 2 * wide),
            *scatter_bufs(rows, wide),
            pltpu.VMEM((chunks, rows, wide), BF16),
            pltpu.VMEM((chunks, rows, 2 * wide), BF16),
            pltpu.VMEM((max(rows, 2 * first), feats), F32),
            pltpu.VMEM((n_col, td, feats), BF16),
            pltpu.VMEM((n_col - 1, td, feats), BF16),
            pltpu.SemaphoreType.DMA((2, n_col - 1)),
            pltpu.SemaphoreType.DMA((2, 2, 2, n_col - 1)),
            pltpu.SemaphoreType.DMA((2, k, chunks)),
            pltpu.SemaphoreType.DMA((2, k, chunks)),
            pltpu.SemaphoreType.DMA((2, k, chunks)),
            pltpu.SemaphoreType.DMA((2, k, chunks)),
            pltpu.SemaphoreType.DMA((2, k, chunks)),
            pltpu.SemaphoreType.DMA((2, n_col - 1)),
            pltpu.SemaphoreType.DMA((2, chunks)),
            pltpu.SemaphoreType.DMA((2, plan.n_dp, 2)),
        ],
        compiler_params=pltpu.CompilerParams(
            collective_id=0, has_side_effects=True, vmem_limit_bytes=63 * 2**20
        ),
    )(cnt, tokens, cotangent, gate_mask, up_mask, down_mask, wg, wu, wd)


def grads_kernel(
    plan, gate_mask, up_mask, down_mask, tokc, gc, hid, dd, gate_grad, up_grad, down_grad, turned
):
    u = pl.program_id(0)
    wide = plan.wide
    side, parts = plan.feats // BLOCK, wide // BLOCK

    @pl.when((u == 0) | (u == plan.per_path))
    def _():
        turned[...] = tokc[0].T

    def keep(mask, value):
        return jnp.where(mask > 0, value, 0.0)

    for ref, mask, lo in ((gate_grad, gate_mask, 0), (up_grad, up_mask, wide)):
        value = jnp.dot(turned[...], dd[0, :, lo : lo + wide], preferred_element_type=F32)
        for r in range(side):
            for c in range(parts):
                rs, cs = slice(r * BLOCK, (r + 1) * BLOCK), slice(c * BLOCK, (c + 1) * BLOCK)
                ref[rs, cs] = keep(mask[r, u * parts + c], value[rs, cs])
    value = jnp.dot(hid[0].T, gc[0], preferred_element_type=F32)
    for r in range(side):
        for c in range(parts):
            rs, cs = slice(r * BLOCK, (r + 1) * BLOCK), slice(c * BLOCK, (c + 1) * BLOCK)
            down_grad[cs, rs] = keep(down_mask[r, u * parts + c], value[cs, rs])


def grads(plan, gate_mask, up_mask, down_mask, tokc, gc, hid, dd):
    rows, feats, wide, per = plan.rows, plan.feats, plan.wide, plan.per_path
    smem = pl.BlockSpec(memory_space=pltpu.SMEM)
    return pl.pallas_call(
        functools.partial(grads_kernel, plan),
        grid=(plan.chunks,),
        out_shape=(
            jax.ShapeDtypeStruct((feats, plan.units), F32),
            jax.ShapeDtypeStruct((feats, plan.units), F32),
            jax.ShapeDtypeStruct((plan.units, feats), F32),
        ),
        in_specs=[
            smem,
            smem,
            smem,
            pl.BlockSpec((1, rows, feats), lambda u: (u // per, 0, 0)),
            pl.BlockSpec((1, rows, feats), lambda u: (u // per, 0, 0)),
            pl.BlockSpec((1, rows, wide), lambda u: (u, 0, 0)),
            pl.BlockSpec((1, rows, 2 * wide), lambda u: (u, 0, 0)),
        ],
        out_specs=(
            pl.BlockSpec((feats, wide), lambda u: (0, u)),
            pl.BlockSpec((feats, wide), lambda u: (0, u)),
            pl.BlockSpec((wide, feats), lambda u: (u, 0)),
        ),
        scratch_shapes=[pltpu.VMEM((feats, rows), BF16)],
        compiler_params=pltpu.CompilerParams(vmem_limit_bytes=63 * 2**20),
    )(gate_mask, up_mask, down_mask, tokc, gc, hid, dd)


def on_device(
    n_col, n_dp,
    tokens, cotangent, gate_weight, up_weight, down_weight, gate_mask, up_mask, down_mask, counts
):
    plan = Plan(n_col, n_dp, tokens.shape[0], tokens.shape[1], gate_weight.shape[1])
    cnt = jnp.broadcast_to(counts.reshape(1, 1), (8, 128))
    down_mask = down_mask.T
    output, tokc, gc, hid, dd = exchange(
        plan, cnt, tokens, cotangent, gate_mask, up_mask, down_mask,
        gate_weight, up_weight, down_weight,
    )
    gate_grad, up_grad, down_grad = grads(plan, gate_mask, up_mask, down_mask, tokc, gc, hid, dd)
    return (output, gate_grad, up_grad, down_grad)


def solution(mesh):
    in_specs = (
        P("col", "dp"),
        P("col", "dp"),
        P("dp", "col"),
        P("dp", "col"),
        P("col", "dp"),
        P("dp", "col"),
        P("dp", "col"),
        P("col", "dp"),
        P("col"),
    )
    out_specs = (P("col", "dp"), P("dp", "col"), P("dp", "col"), P("col", "dp"))
    return jax.shard_map(
        functools.partial(on_device, mesh.shape["col"], mesh.shape["dp"]),
        mesh=mesh,
        in_specs=in_specs,
        out_specs=out_specs,
        check_vma=False,
    )
```
